128 devices in a mesh: ex: 8 (over x, core), qry: 16 (over y, z).
Axes of the slice: x: 4, y: 4, z: 4, core: 2. Of those that a mesh axis runs over, the one named last changes fastest.
Arguments:
- train_proj: bfloat16 [16384, 4096], P('ex', 'qry'), may hold values from -6 to 6
- query_proj: bfloat16 [8192, 4096], P('qry', 'ex'), may hold values from -0.09375 to 0.09375
- out_weight: float32 [16384], P('ex'), may hold values from 0.1 to 1
- train_feat: float32 [16384, 16384], P('qry', 'ex'), may hold values from -6 to 6
- query_feat: float32 [8192, 16384], P('qry', 'ex'), may hold values from -0.046875 to 0.046875
- candidates: int32 [64, 2], replicated, may hold values from 0 to 127, as said below
Outputs:
- scores: float32 [16384, 8192], P('ex', 'qry')
- exact: float32 [64, 2, 128, 128], P('qry', None, 'ex')
The draws below stay inside these ranges and needn't reach their ends.
Inputs may be any that keep to these rules, and one draw needn't show every extreme that they name: `candidates`: split the training rows into equal ranges, one for each qry index in order. The 8 entries of the tiles of one qry index name blocks in pairwise different ranges; some ranges are named far more often than others.
All inputs are finite; a program needn't handle non-finite values.
Results may differ from the reference program's by a relative error of at most 0.0003.
Values may be sent and summed in bfloat16 or wider, within the bound.
A program may use at most 192 MiB of HBM per device.

```python
import math
import jax
import jax.numpy as jnp
from jax import lax

PROJ_WIDTH = 4096
FEAT_WIDTH = 16384
BLOCK_ROWS = 128
CANDS = 2
TRAIN_ROWS = 16384
QUERIES = 8192
TILES = 64
TILES_DEV = 4
N_QRY = 16


def draw_candidates(key, part):
    key = jax.random.fold_in(key, 11)
    key_pop, key_noise, key_order, key_offset = jax.random.split(key, 4)
    per_device = TILES_DEV * CANDS
    popular = jax.random.randint(key_pop, (N_QRY,), 0, 4)
    noise = jax.random.randint(key_noise, (N_QRY, N_QRY), 0, 3)
    ranking = (popular[None, :] + noise) * N_QRY + jnp.arange(N_QRY)[None, :]
    chosen = lax.top_k(ranking, per_device)[1]
    order_keys = jax.random.split(key_order, N_QRY)
    shuffled = jax.vmap(lambda k, row: jax.random.permutation(k, row))(order_keys, chosen)
    per_owner = TRAIN_ROWS // (BLOCK_ROWS * N_QRY)
    offsets = jax.random.randint(key_offset, (N_QRY, per_device), 0, per_owner)
    blocks = shuffled * per_owner + offsets
    return blocks.reshape(TILES, CANDS).astype(jnp.int32)


def shard_levels(rng, shape, pieces, smallest, top_value):
    loudness = 1.0
    for dim, blocks in pieces:
        steps = jax.random.uniform(jax.random.fold_in(jax.random.fold_in(rng, 6), dim), (blocks,), jnp.float32, smallest / len(pieces), top_value / len(pieces))
        loudness = loudness * jnp.repeat(jnp.exp(steps), shape[dim] // blocks).reshape((-1,) + (1,) * (len(shape) - 1 - dim))
    return loudness


def scatter_about(own_key, shape, width, bound, shards=(), dtype=jnp.bfloat16):
    values = width * jax.random.normal(own_key, shape, jnp.float32)
    if shards:
        values = values * shard_levels(own_key, shape, shards, -0.22, 0.18)
    return jnp.clip(values, -bound, bound).astype(dtype)


def setup_inputs(seed: int = 0) -> dict:
    keys = jax.random.split(jax.random.key(seed), 7)
    train_proj = scatter_about(keys[0], (TRAIN_ROWS, PROJ_WIDTH), 1.0, 6.0, ((0, 8), (1, 16)))
    query_proj = scatter_about(keys[1], (QUERIES, PROJ_WIDTH), PROJ_WIDTH ** -0.5, 0.09375, ((0, 16), (1, 8)))
    out_weight = jnp.clip(jnp.exp(math.log(1.0) - 2.3025851 * jax.random.uniform(keys[2], (TRAIN_ROWS,), jnp.float32) ** shard_levels(keys[2], (TRAIN_ROWS,), ((0, 8),), -0.2, 0.2)), 0.1, 1.0)
    train_feat = scatter_about(keys[3], (TRAIN_ROWS, FEAT_WIDTH), 1.0, 6.0, ((0, 16), (1, 8)), jnp.float32)
    query_feat = scatter_about(keys[4], (QUERIES, FEAT_WIDTH), FEAT_WIDTH ** -0.5, 0.046875, ((0, 16), (1, 8)), jnp.float32)
    candidates = draw_candidates(jax.random.fold_in(keys[6], 71), 0)
    return dict(train_proj=train_proj, query_proj=query_proj, out_weight=out_weight, train_feat=train_feat, query_feat=query_feat, candidates=candidates)


def reference(train_proj, query_proj, out_weight, train_feat, query_feat, candidates):
    slabs = train_proj.reshape(TRAIN_ROWS // 256, 256, PROJ_WIDTH)

    def score_slab(slab):
        return jnp.dot(slab, query_proj.T, preferred_element_type=jnp.float32)

    products = lax.map(score_slab, slabs).reshape(TRAIN_ROWS, QUERIES)
    scores = products * out_weight[:, None]
    block_ids = candidates.reshape(-1).astype(jnp.int32)
    tile_ids = (jnp.arange(TILES * CANDS) // CANDS).astype(jnp.int32)

    def rescore(pair):
        block, tile = pair
        rows = lax.dynamic_slice_in_dim(train_feat, (block * BLOCK_ROWS).astype(jnp.int32), BLOCK_ROWS, 0)
        picked = lax.dynamic_slice_in_dim(query_feat, (tile * BLOCK_ROWS).astype(jnp.int32), BLOCK_ROWS, 0)
        return jnp.dot(rows, picked.T, precision=lax.Precision.HIGHEST)

    exact = lax.map(rescore, (block_ids, tile_ids)).reshape(TILES, CANDS, BLOCK_ROWS, BLOCK_ROWS)
    return scores, exact
```

```python
import functools

import jax
import jax.numpy as jnp
from jax import lax
from jax.experimental import pallas as pl
from jax.experimental.pallas import tpu as pltpu
from jax.sharding import PartitionSpec as P

BLOCK_ROWS = 128
CANDS = 2
RING = 4
TOP = 32752.0
MESH = pl.DeviceIdType.MESH
MIB = 1 << 20


def code_kernel(pick_ref, rows_ref, codes_ref, scale_ref):
    rows = rows_ref[0]
    top = jnp.maximum(jnp.max(jnp.abs(rows), axis=1, keepdims=True), 1e-30)
    codes_ref[0] = jnp.round(rows * (TOP / top)).astype(jnp.int32).astype(jnp.int16)
    wide = jnp.broadcast_to(top * (1.0 / TOP), (BLOCK_ROWS, BLOCK_ROWS))
    scale_ref[0] = jnp.transpose(wide)[:8]


def code_slots(pick, train_feat):
    slots = pick.shape[0]
    held, width = train_feat.shape[0] // BLOCK_ROWS, train_feat.shape[1]
    blocks = train_feat.reshape(held, BLOCK_ROWS, width)
    return pl.pallas_call(
        code_kernel,
        grid_spec=pltpu.PrefetchScalarGridSpec(
            num_scalar_prefetch=1,
            grid=(slots,),
            in_specs=[pl.BlockSpec((1, BLOCK_ROWS, width), lambda d, pick: (pick[d], 0, 0))],
            out_specs=[
                pl.BlockSpec((1, BLOCK_ROWS, width), lambda d, pick: (d, 0, 0)),
                pl.BlockSpec((1, 8, BLOCK_ROWS), lambda d, pick: (d, 0, 0)),
            ],
        ),
        out_shape=[
            jax.ShapeDtypeStruct((slots, BLOCK_ROWS, width), jnp.int16),
            jax.ShapeDtypeStruct((slots, 8, BLOCK_ROWS), jnp.float32),
        ],
        compiler_params=pltpu.CompilerParams(vmem_limit_bytes=24 * MIB),
        name="code_slots",
    )(pick, blocks)


def main_kernel(
    owner_ref, train_ref, query_ref, tiles_ref, codes_ref, scale_ref,
    prod_ref, exact_ref,
    pieces, queries, slots, slot_scale, split, parts, parts_in,
    own_sem, ring_send, ring_recv, query_send, query_recv, slot_send, slot_recv, part_send, part_recv,
):
    ex, qry = lax.axis_index("ex"), lax.axis_index("qry")
    n_ex, n_qry = queries.shape[0], slots.shape[0]
    y, z = qry // RING, qry % RING
    turn = lambda a, d: (a + d) % RING
    at = {
        "y+": turn(y, 1) * RING + z,
        "y-": turn(y, 3) * RING + z,
        "z+": y * RING + turn(z, 1),
        "z-": y * RING + turn(z, 3),
    }

    own = [
        pltpu.make_async_copy(train_ref, pieces.at[0], own_sem.at[0]),
        pltpu.make_async_copy(query_ref, queries.at[ex], own_sem.at[1]),
        pltpu.make_async_copy(codes_ref.at[qry], slots.at[qry], own_sem.at[2]),
        pltpu.make_async_copy(scale_ref.at[qry], slot_scale.at[qry], own_sem.at[3]),
    ]
    for copy in own:
        copy.start()

    barrier = pltpu.get_barrier_semaphore()
    for d in range(1, n_qry):
        there = turn(y, d // RING) * RING + turn(z, d % RING)
        pl.semaphore_signal(barrier, inc=1, device_id={"qry": there}, device_id_type=MESH)
    for d in range(1, n_ex):
        pl.semaphore_signal(barrier, inc=1, device_id={"ex": (ex + d) % n_ex}, device_id_type=MESH)
    pl.semaphore_wait(barrier, n_qry - 1 + n_ex - 1)

    sent = []
    arriving = {}
    count = [0]

    def move(source, target, way):
        (piece, quarter, many), (new_piece, _, _) = source, target
        k = count[0]
        count[0] += 1
        src = train_ref if piece == 0 else pieces.at[piece]
        copy = pltpu.make_async_remote_copy(
            src_ref=src.at[pl.ds(quarter, many)],
            dst_ref=pieces.at[new_piece, pl.ds(quarter, many)],
            send_sem=ring_send.at[k],
            recv_sem=ring_recv.at[k],
            device_id={"qry": at[way]},
            device_id_type=MESH,
        )
        copy.start()
        sent.append(copy)
        arriving[target] = copy

    def landed(*targets):
        for target in targets:
            arriving[target].wait_recv()

    rel = lambda dy, dz: dy * RING + dz

    move((0, 0, 2), (rel(0, 1), 0, 2), "z+")
    move((0, 0, 2), (rel(0, 3), 0, 2), "z-")
    move((0, 2, 2), (rel(1, 0), 2, 2), "y+")
    move((0, 2, 2), (rel(3, 0), 2, 2), "y-")

    slot_copies = []
    for d in range(1, n_qry):
        there = turn(y, d // RING) * RING + turn(z, d % RING)
        for j, (src, dst) in enumerate(((codes_ref, slots), (scale_ref, slot_scale))):
            copy = pltpu.make_async_remote_copy(
                src_ref=src.at[there],
                dst_ref=dst.at[qry],
                send_sem=slot_send.at[j, d],
                recv_sem=slot_recv.at[j, d],
                device_id={"qry": there},
                device_id_type=MESH,
            )
            copy.start()
            slot_copies.append(copy)

    query_copies = []
    for d in range(1, n_ex):
        copy = pltpu.make_async_remote_copy(
            src_ref=query_ref,
            dst_ref=queries.at[ex],
            send_sem=query_send.at[d],
            recv_sem=query_recv.at[d],
            device_id={"ex": (ex + d) % n_ex},
            device_id_type=MESH,
        )
        copy.start()
        query_copies.append(copy)

    def second(piece_of, quarter, ways):
        move((piece_of(0), quarter, 2), (piece_of(1), quarter, 2), ways[0])
        move((piece_of(0), quarter, 2), (piece_of(3), quarter, 2), ways[1])

    def along_y(dz):
        return lambda dy: rel(dy, dz)

    def along_z(dy):
        return lambda dz: rel(dy, dz)

    second(along_y(0), 0, ("y+", "y-"))
    second(along_z(0), 2, ("z+", "z-"))

    @pl.loop(0, split.shape[1])
    def _(t):
        whole = tiles_ref[t]
        high = whole.astype(jnp.bfloat16)
        split[0, t] = high
        split[1, t] = (whole - high.astype(jnp.float32)).astype(jnp.bfloat16)

    for copy in own:
        copy.wait()
    for copy in query_copies:
        copy.wait_recv()

    def multiply(piece, quarter, first=False):
        dy, dz = piece // RING, piece % RING
        column = turn(y, RING - dy) * RING + turn(z, RING - dz)
        block = queries[column // 2, :, pl.ds(pl.multiple_of((column % 2) * 256, 256), 256)]
        for k in range(quarter, quarter + 2):
            value = lax.dot_general(
                pieces[piece, k], block, (((1,), (1,)), ((), ())), preferred_element_type=jnp.float32
            )
            if first:
                prod_ref[k] = value
            else:
                prod_ref[k] += value

    multiply(0, 0, True)
    multiply(0, 2, True)

    def relay(piece, quarter, new_piece, way):
        move((piece, quarter, 1), (new_piece, quarter, 1), way)

    for d, wz, wy, k in ((1, "z+", "y+", 0), (3, "z-", "y-", 1)):
        landed((rel(0, d), 0, 2))
        relay(rel(0, d), k, rel(0, 2), wz)
        second(along_y(d), 0, ("y+", "y-"))
        landed((rel(d, 0), 2, 2))
        relay(rel(d, 0), 2 + k, rel(2, 0), wy)
        second(along_z(d), 2, ("z+", "z-"))
        multiply(rel(0, d), 0)
        multiply(rel(d, 0), 2)
    for k in range(2):
        landed((rel(0, 2), k, 1))
        landed((rel(2, 0), 2 + k, 1))
    second(along_y(2), 0, ("y+", "y-"))
    second(along_z(2), 2, ("z+", "z-"))
    multiply(rel(0, 2), 0)
    multiply(rel(2, 0), 2)

    def pass_on(c):
        for d, wy, wz, k in ((1, "y+", "z+", 0), (3, "y-", "z-", 1)):
            landed((rel(d, c), 0, 2))
            relay(rel(d, c), k, rel(2, c), wy)
            landed((rel(c, d), 2, 2))
            relay(rel(c, d), 2 + k, rel(c, 2), wz)
            multiply(rel(d, c), 0)
            multiply(rel(c, d), 2)

    def finish(c):
        for k in range(2):
            landed((rel(2, c), k, 1))
            landed((rel(c, 2), 2 + k, 1))
        multiply(rel(2, c), 0)
        multiply(rel(c, 2), 2)

    pass_on(0)
    pass_on(1)
    finish(0)
    pass_on(3)
    finish(1)
    pass_on(2)

    for copy in slot_copies:
        copy.wait_recv()

    pairs = parts.shape[1]
    width = slots.shape[2]
    step = 512

    @pl.loop(0, pairs)
    def _(p):
        slot = owner_ref[p]
        tile = p // CANDS
        total = jnp.zeros((BLOCK_ROWS, BLOCK_ROWS), jnp.float32)
        for c in range(0, width, step):
            rows = slots[slot, :, c : c + step].astype(jnp.float32)
            high = rows.astype(jnp.bfloat16)
            low = (rows - high.astype(jnp.float32)).astype(jnp.bfloat16)
            tile_high, tile_low = split[0, tile, :, c : c + step], split[1, tile, :, c : c + step]
            for a, b in ((high, tile_high), (high, tile_low), (low, tile_high)):
                total += lax.dot_general(a, b, (((1,), (1,)), ((), ())), preferred_element_type=jnp.float32)
        tall = jnp.transpose(jnp.broadcast_to(slot_scale[slot][:1], (BLOCK_ROWS, BLOCK_ROWS)))
        parts[:, p] = (total * tall).reshape(parts.shape[0], parts.shape[2], BLOCK_ROWS)

    part_copies = []
    for d in range(1, n_ex):
        there = (ex + d) % n_ex
        copy = pltpu.make_async_remote_copy(
            src_ref=parts.at[there],
            dst_ref=parts_in.at[d],
            send_sem=part_send.at[d],
            recv_sem=part_recv.at[d],
            device_id={"ex": there},
            device_id_type=MESH,
        )
        copy.start()
        part_copies.append(copy)

    finish(3)
    total = parts[ex]
    for d, copy in enumerate(part_copies, 1):
        copy.wait_recv()
        total += parts_in[d]
    exact_ref[...] = total
    finish(2)

    for copy in sent + slot_copies + query_copies + part_copies:
        copy.wait_send()


def local(train_proj, query_proj, out_weight, train_feat, query_feat, candidates):
    n_qry, n_ex = lax.axis_size("qry"), lax.axis_size("ex")
    my_index = lax.axis_index("qry")
    width = train_feat.shape[1]
    held_blocks = train_feat.shape[0] // BLOCK_ROWS
    tiles_here = query_feat.shape[0] // BLOCK_ROWS
    pairs = tiles_here * CANDS
    items = candidates.reshape(n_qry, pairs)
    wanted_here = items // held_blocks == my_index
    pick = jnp.sum(jnp.where(wanted_here, items % held_blocks, 0), axis=1)
    my_owner = lax.dynamic_slice_in_dim(items, my_index, 1, 0)[0] // held_blocks
    codes, scale = code_slots(pick, train_feat)

    rows, depth = train_proj.shape
    columns, part_depth = query_proj.shape
    share = BLOCK_ROWS // n_ex
    any_space, vmem = pl.BlockSpec(memory_space=pl.ANY), pl.BlockSpec(memory_space=pltpu.VMEM)
    dma = pltpu.SemaphoreType.DMA
    products, exact = pl.pallas_call(
        main_kernel,
        out_shape=[
            jax.ShapeDtypeStruct((4, rows // 4, columns), jnp.float32),
            jax.ShapeDtypeStruct((pairs, share, BLOCK_ROWS), jnp.float32),
        ],
        in_specs=[pl.BlockSpec(memory_space=pltpu.SMEM), any_space, any_space, vmem, any_space, any_space],
        out_specs=[vmem, vmem],
        scratch_shapes=[
            pltpu.VMEM((n_qry, 4, rows // 4, depth), jnp.bfloat16),
            pltpu.VMEM((n_ex, columns, part_depth), jnp.bfloat16),
            pltpu.VMEM((n_qry, BLOCK_ROWS, width), jnp.int16),
            pltpu.VMEM((n_qry, 8, BLOCK_ROWS), jnp.float32),
            pltpu.VMEM((2, tiles_here, BLOCK_ROWS, width), jnp.bfloat16),
            pltpu.VMEM((n_ex, pairs, share, BLOCK_ROWS), jnp.float32),
            pltpu.VMEM((n_ex, pairs, share, BLOCK_ROWS), jnp.float32),
            dma((4,)),
            dma((40,)),
            dma((40,)),
            dma((n_ex,)),
            dma((n_ex,)),
            dma((2, n_qry)),
            dma((2, n_qry)),
            dma((n_ex,)),
            dma((n_ex,)),
        ],
        compiler_params=pltpu.CompilerParams(
            collective_id=0, has_side_effects=True, vmem_limit_bytes=58 * MIB
        ),
        name="main",
    )(
        my_owner,
        train_proj.reshape(4, rows // 4, depth),
        query_proj,
        query_feat.reshape(tiles_here, BLOCK_ROWS, width),
        codes,
        scale,
    )
    scores = products.reshape(rows, columns) * out_weight[:, None]
    return scores, exact.reshape(tiles_here, CANDS, share, BLOCK_ROWS)


def solution(mesh):
    placed = (P("ex", "qry"), P("qry", "ex"), P("ex"), P("qry", "ex"), P("qry", "ex"), P())
    return jax.shard_map(
        local,
        mesh=mesh,
        in_specs=placed,
        out_specs=(P("ex", "qry"), P("qry", None, "ex", None)),
        check_vma=False,
    )
```

```python
import functools

import jax
import jax.numpy as jnp
from jax import lax
from jax.experimental import pallas as pl
from jax.experimental.pallas import tpu as pltpu
from jax.sharding import PartitionSpec as P

BLOCK_ROWS = 128
CANDS = 2
RING = 4
SLOT_CHUNKS = 4
COPIES = 144
TOP = 32752.0
MESH = pl.DeviceIdType.MESH
MIB = 1 << 20


def code_kernel(pick_ref, rows_ref, codes_ref, scale_ref):
    rows = rows_ref[0]
    top = jnp.maximum(jnp.max(jnp.abs(rows), axis=1, keepdims=True), 1e-30)
    codes_ref[0] = jnp.round(rows * (TOP / top)).astype(jnp.int32).astype(jnp.int16)
    wide = jnp.broadcast_to(top * (1.0 / TOP), (BLOCK_ROWS, BLOCK_ROWS))
    scale_ref[0] = jnp.transpose(wide)[:8]


def code_slots(pick, train_feat):
    slots = pick.shape[0]
    held, width = train_feat.shape[0] // BLOCK_ROWS, train_feat.shape[1]
    blocks = train_feat.reshape(held, BLOCK_ROWS, width)
    return pl.pallas_call(
        code_kernel,
        grid_spec=pltpu.PrefetchScalarGridSpec(
            num_scalar_prefetch=1,
            grid=(slots,),
            in_specs=[pl.BlockSpec((1, BLOCK_ROWS, width), lambda d, pick: (pick[d], 0, 0))],
            out_specs=[
                pl.BlockSpec((1, BLOCK_ROWS, width), lambda d, pick: (d, 0, 0)),
                pl.BlockSpec((1, 8, BLOCK_ROWS), lambda d, pick: (d, 0, 0)),
            ],
        ),
        out_shape=[
            jax.ShapeDtypeStruct((slots, BLOCK_ROWS, width), jnp.int16),
            jax.ShapeDtypeStruct((slots, 8, BLOCK_ROWS), jnp.float32),
        ],
        compiler_params=pltpu.CompilerParams(vmem_limit_bytes=24 * MIB),
        name="code_slots",
    )(pick, blocks)


def main_kernel(
    owner_ref, train_ref, query_ref, tiles_ref, codes_ref, scale_ref,
    out_ref, out_scale_ref, exact_ref,
    trains, queries, slots, slot_scale, tiles, split, products, ready, ready_scale, parts, parts_in,
    own_sem, send_sem, recv_sem,
):
    ex, qry = lax.axis_index("ex"), lax.axis_index("qry")
    n_ex, n_qry = parts.shape[0], slots.shape[0]
    x, core, y, z = ex // 2, ex % 2, qry // RING, qry % RING
    turn = lambda a, d: (a + d) % RING
    sent = []

    def send(src, dst, dx=0, dc=0, dy=0, dz=0):
        there = {"ex": turn(x, dx) * 2 + (core + dc) % 2, "qry": turn(y, dy) * RING + turn(z, dz)}
        k = len(sent)
        copy = pltpu.make_async_remote_copy(
            src_ref=src,
            dst_ref=dst,
            send_sem=send_sem.at[k],
            recv_sem=recv_sem.at[k],
            device_id=there,
            device_id_type=MESH,
        )
        copy.start()
        sent.append(copy)
        return copy

    rows, width = trains.shape[1], slots.shape[2]
    depth, part_depth = train_ref.shape[2], query_ref.shape[1]
    half = rows // 2
    my_depth = pl.ds(pl.multiple_of(z * depth, depth), depth)
    my_part = pl.ds(pl.multiple_of(core * part_depth, part_depth), part_depth)

    own = [
        pltpu.make_async_copy(train_ref.at[z], trains.at[y, :, my_depth], own_sem.at[0]),
        pltpu.make_async_copy(query_ref, queries.at[x, z, :, my_part], own_sem.at[1]),
        pltpu.make_async_copy(codes_ref.at[qry], slots.at[qry], own_sem.at[2]),
        pltpu.make_async_copy(scale_ref.at[qry], slot_scale.at[qry], own_sem.at[3]),
        pltpu.make_async_copy(tiles_ref, tiles, own_sem.at[4]),
    ]
    for copy in own:
        copy.start()

    barrier = pltpu.get_barrier_semaphore()
    for d in range(1, n_qry):
        there = turn(y, d // RING) * RING + turn(z, d % RING)
        pl.semaphore_signal(barrier, inc=1, device_id={"qry": there}, device_id_type=MESH)
    for d in range(1, n_ex):
        there = turn(x, d // 2) * 2 + (core + d % 2) % 2
        pl.semaphore_signal(barrier, inc=1, device_id={"ex": there}, device_id_type=MESH)
    pl.semaphore_wait(barrier, n_qry - 1 + n_ex - 1)

    def query_half(at_x, at_z, h):
        return queries.at[at_x, at_z, pl.ds(h * half, half), my_part]

    def query_sends(source, at_z):
        out = {}
        for h in range(2):
            for d in (1, 3):
                out[d, h] = send(source(h), query_half(x, at_z, h), dx=d)
        return out

    near_z = {}
    for h in range(2):
        for d in (1, 3):
            near_z[d, h] = send(query_ref.at[pl.ds(h * half, half)], query_half(x, z, h), dz=d)
    along_x = {0: query_sends(lambda h: query_ref.at[pl.ds(h * half, half)], z)}
    train_z = [
        send(train_ref.at[turn(z, d)], trains.at[y, :, my_depth], dz=d) for d in (1, 3, 2)
    ]

    slot_copies = []
    order = ((0, 1), (1, 0), (0, 3), (3, 0), (1, 1), (3, 3), (1, 3), (3, 1), (2, 1), (1, 2), (2, 3), (3, 2), (0, 2), (2, 0), (2, 2))
    chunk = BLOCK_ROWS // SLOT_CHUNKS

    def slot_round(r):
        for dy, dz in order:
            there = turn(y, dy) * RING + turn(z, dz)
            if r == 0:
                slot_copies.append(send(scale_ref.at[there], slot_scale.at[qry], dy=dy, dz=dz))
            part = pl.ds(r * chunk, chunk)
            slot_copies.append(send(codes_ref.at[there, part], slots.at[qry, part], dy=dy, dz=dz))

    slot_round(0)

    near_z[1, 0].wait_recv()
    far_z = {0: send(query_half(x, turn(z, 3), 0), query_half(x, turn(z, 3), 0), dz=1)}
    near_z[3, 1].wait_recv()
    far_z[1] = send(query_half(x, turn(z, 1), 1), query_half(x, turn(z, 1), 1), dz=3)
    near_z[1, 1].wait_recv()
    along_x[3] = query_sends(lambda h: query_half(x, turn(z, 3), h), turn(z, 3))
    near_z[3, 0].wait_recv()
    along_x[1] = query_sends(lambda h: query_half(x, turn(z, 1), h), turn(z, 1))

    for copy in train_z:
        copy.wait_recv()
    own[0].wait()

    def train_half(at_y, h):
        return trains.at[at_y, pl.ds(h * half, half)]

    near_y = {}
    for h in range(2):
        for d in (1, 3):
            near_y[d, h] = send(train_half(y, h), train_half(y, h), dy=d)
    slot_round(1)

    def relay_x(d):
        at_z = turn(z, d)
        along_x[d][1, 0].wait_recv()
        first = send(query_half(turn(x, 3), at_z, 0), query_half(turn(x, 3), at_z, 0), dx=1)
        along_x[d][3, 1].wait_recv()
        second = send(query_half(turn(x, 1), at_z, 1), query_half(turn(x, 1), at_z, 1), dx=3)
        return first, second

    far_x = {0: relay_x(0)}

    far_z[0].wait_recv()
    far_z[1].wait_recv()
    along_x[2] = query_sends(lambda h: query_half(x, turn(z, 2), h), turn(z, 2))
    own[1].wait()

    def to_core(at_x):
        view = queries.at[at_x, :, :, my_part]
        return send(view, view, dc=1)

    from_core = {0: to_core(x)}

    near_y[1, 0].wait_recv()
    far_y = {0: send(train_half(turn(y, 3), 0), train_half(turn(y, 3), 0), dy=1)}
    near_y[3, 1].wait_recv()
    far_y[1] = send(train_half(turn(y, 1), 1), train_half(turn(y, 1), 1), dy=3)
    slot_round(2)

    own[4].wait()

    @pl.loop(0, split.shape[1])
    def _(t):
        whole = tiles[t]
        high = whole.astype(jnp.bfloat16)
        split[0, t] = high
        split[1, t] = (whole - high.astype(jnp.float32)).astype(jnp.bfloat16)

    far_x[3] = relay_x(3)
    far_x[1] = relay_x(1)
    slot_round(3)
    near_y[1, 1].wait_recv()
    near_y[3, 0].wait_recv()
    far_y[0].wait_recv()
    far_y[1].wait_recv()

    def multiply(at_x, first=False):
        from_core[at_x].wait_recv()
        place = turn(x, at_x)

        @pl.loop(0, RING)
        def _(to):
            value = lax.dot_general(
                trains[place], queries[place, to], (((1,), (1,)), ((), ())), preferred_element_type=jnp.float32
            )
            if first:
                products[to] = value
            else:
                products[to] += value

    multiply(0, True)
    far_x[2] = relay_x(2)
    for d in range(RING):
        along_x[d][1, 1].wait_recv()
        along_x[d][3, 0].wait_recv()
    from_core[3] = to_core(turn(x, 3))
    from_core[1] = to_core(turn(x, 1))
    multiply(3)
    multiply(1)
    for d in range(RING):
        far_x[d][0].wait_recv()
        far_x[d][1].wait_recv()
    from_core[2] = to_core(turn(x, 2))
    multiply(2)

    @pl.loop(0, RING)
    def _(to):
        value = products[to]
        top = jnp.maximum(jnp.max(jnp.abs(value), axis=1, keepdims=True), 1e-30)
        ready[to] = jnp.round(value * (TOP / top)).astype(jnp.int32).astype(jnp.int16)
        ready_scale[to] = jnp.transpose(jnp.broadcast_to(top * (1.0 / TOP), (rows, 128)))[:8]

    out_copies = []
    for d in (1, 3, 2):
        out_copies.append(send(ready_scale.at[turn(z, d)], out_scale_ref.at[z], dz=d))
        for h in range(2):
            part = pl.ds(h * half, half)
            out_copies.append(send(ready.at[turn(z, d), part], out_ref.at[z, part], dz=d))
    stay = [
        pltpu.make_async_copy(ready.at[z], out_ref.at[z], own_sem.at[5]),
        pltpu.make_async_copy(ready_scale.at[z], out_scale_ref.at[z], own_sem.at[6]),
    ]
    for copy in stay:
        copy.start()

    own[2].wait()
    own[3].wait()
    for copy in slot_copies:
        copy.wait_recv()
    step = 512

    @pl.loop(0, parts.shape[1])
    def _(p):
        slot = owner_ref[p]
        tile = p // CANDS
        total = jnp.zeros((BLOCK_ROWS, BLOCK_ROWS), jnp.float32)
        for c in range(0, width, step):
            block = slots[slot, :, c : c + step].astype(jnp.float32)
            high = block.astype(jnp.bfloat16)
            low = (block - high.astype(jnp.float32)).astype(jnp.bfloat16)
            tile_high, tile_low = split[0, tile, :, c : c + step], split[1, tile, :, c : c + step]
            for a, b in ((high, tile_high), (high, tile_low), (low, tile_high)):
                total += lax.dot_general(a, b, (((1,), (1,)), ((), ())), preferred_element_type=jnp.float32)
        tall = jnp.transpose(jnp.broadcast_to(slot_scale[slot][:1], (BLOCK_ROWS, BLOCK_ROWS)))
        parts[:, p] = (total * tall).reshape(parts.shape[0], parts.shape[2], BLOCK_ROWS)

    part_copies = []
    for d in range(1, n_ex):
        there = turn(x, d // 2) * 2 + (core + d % 2) % 2
        part_copies.append(send(parts.at[there], parts_in.at[d], dx=d // 2, dc=d % 2))
    total = parts[ex]
    for d, copy in enumerate(part_copies, 1):
        copy.wait_recv()
        total += parts_in[d]
    exact_ref[...] = total

    for copy in out_copies:
        copy.wait_recv()
    for copy in stay:
        copy.wait()
    for copy in sent:
        copy.wait_send()


def decode_kernel(codes_ref, scale_ref, weight_ref, scores_ref):
    line = scale_ref[0][:1] * weight_ref[0]
    tall = jnp.transpose(jnp.broadcast_to(line, (128, line.shape[1])))
    scores_ref[...] = codes_ref[0].astype(jnp.float32) * tall[:, :1]


def local(train_proj, query_proj, out_weight, train_feat, query_feat, candidates):
    n_qry, n_ex = lax.axis_size("qry"), lax.axis_size("ex")
    my_index = lax.axis_index("qry")
    width = train_feat.shape[1]
    held_blocks = train_feat.shape[0] // BLOCK_ROWS
    tiles_here = query_feat.shape[0] // BLOCK_ROWS
    pairs = tiles_here * CANDS
    items = candidates.reshape(n_qry, pairs)
    wanted_here = items // held_blocks == my_index
    pick = jnp.sum(jnp.where(wanted_here, items % held_blocks, 0), axis=1)
    my_owner = lax.dynamic_slice_in_dim(items, my_index, 1, 0)[0] // held_blocks
    codes, scale = code_slots(pick, train_feat)

    depth = train_proj.shape[1]
    rows = train_proj.shape[0] // RING
    columns, part_depth = query_proj.shape
    share = BLOCK_ROWS // n_ex
    any_space, vmem = pl.BlockSpec(memory_space=pl.ANY), pl.BlockSpec(memory_space=pltpu.VMEM)
    dma = pltpu.SemaphoreType.DMA
    result, result_scale, exact = pl.pallas_call(
        main_kernel,
        out_shape=[
            jax.ShapeDtypeStruct((RING, rows, columns), jnp.int16),
            jax.ShapeDtypeStruct((RING, 8, rows), jnp.float32),
            jax.ShapeDtypeStruct((pairs, share, BLOCK_ROWS), jnp.float32),
        ],
        in_specs=[pl.BlockSpec(memory_space=pltpu.SMEM)] + [any_space] * 5,
        out_specs=[vmem, vmem, vmem],
        scratch_shapes=[
            pltpu.VMEM((RING, rows, RING * depth), jnp.bfloat16),
            pltpu.VMEM((RING, RING, columns, 2 * part_depth), jnp.bfloat16),
            pltpu.VMEM((n_qry, BLOCK_ROWS, width), jnp.int16),
            pltpu.VMEM((n_qry, 8, BLOCK_ROWS), jnp.float32),
            pltpu.VMEM((tiles_here, BLOCK_ROWS, width), jnp.float32),
            pltpu.VMEM((2, tiles_here, BLOCK_ROWS, width), jnp.bfloat16),
            pltpu.VMEM((RING, rows, columns), jnp.float32),
            pltpu.VMEM((RING, rows, columns), jnp.int16),
            pltpu.VMEM((RING, 8, rows), jnp.float32),
            pltpu.VMEM((n_ex, pairs, share, BLOCK_ROWS), jnp.float32),
            pltpu.VMEM((n_ex, pairs, share, BLOCK_ROWS), jnp.float32),
            dma((8,)),
            dma((COPIES,)),
            dma((COPIES,)),
        ],
        compiler_params=pltpu.CompilerParams(
            collective_id=0, has_side_effects=True, vmem_limit_bytes=58 * MIB
        ),
        name="main",
    )(
        my_owner,
        train_proj.reshape(RING, rows, depth),
        query_proj,
        query_feat.reshape(tiles_here, BLOCK_ROWS, width),
        codes,
        scale,
    )
    scores = pl.pallas_call(
        decode_kernel,
        grid=(RING,),
        in_specs=[
            pl.BlockSpec((1, rows, columns), lambda i: (i, 0, 0)),
            pl.BlockSpec((1, 8, rows), lambda i: (i, 0, 0)),
            pl.BlockSpec((1, 1, rows), lambda i: (i, 0, 0)),
        ],
        out_specs=pl.BlockSpec((rows, columns), lambda i: (i, 0)),
        out_shape=jax.ShapeDtypeStruct((RING * rows, columns), jnp.float32),
        compiler_params=pltpu.CompilerParams(vmem_limit_bytes=24 * MIB),
        name="decode",
    )(result, result_scale, out_weight.reshape(RING, 1, rows))
    return scores, exact.reshape(tiles_here, CANDS, share, BLOCK_ROWS)


def solution(mesh):
    placed = (P("ex", "qry"), P("qry", "ex"), P("ex"), P("qry", "ex"), P("qry", "ex"), P())
    return jax.shard_map(
        local,
        mesh=mesh,
        in_specs=placed,
        out_specs=(P("ex", "qry"), P("qry", None, "ex", None)),
        check_vma=False,
    )
```

```python
import jax
import jax.numpy as jnp
from jax import lax
from jax.experimental import pallas as pl
from jax.experimental.pallas import tpu as pltpu
from jax.sharding import PartitionSpec as P

BLOCK_ROWS = 128
CANDS = 2
RING = 4
SLOT_CHUNKS = 4
COPIES = 144
TOP = 32752.0
MESH = pl.DeviceIdType.MESH
MIB = 1 << 20


def main_kernel(
    cand_ref, train_ref, query_ref, blocks_ref, tiles_ref,
    out_ref, out_scale_ref, exact_ref,
    pick, stage, coded, coded_scale, leaving, leaving_scale,
    trains, queries, slots, slot_scale, split, product, ready, ready_scale, parts, parts_in,
    stage_sem, own_sem, send_sem, recv_sem,
):
    ex, qry = lax.axis_index("ex"), lax.axis_index("qry")
    n_ex, n_qry = parts.shape[0], slots.shape[0]
    x, core, y, z = ex // 2, ex % 2, qry // RING, qry % RING
    turn = lambda a, d: (a + d) % RING
    sent = []

    def send(src, dst, dx=0, dc=0, dy=0, dz=0):
        there = {"ex": turn(x, dx) * 2 + (core + dc) % 2, "qry": turn(y, dy) * RING + turn(z, dz)}
        k = len(sent)
        copy = pltpu.make_async_remote_copy(
            src_ref=src,
            dst_ref=dst,
            send_sem=send_sem.at[k],
            recv_sem=recv_sem.at[k],
            device_id=there,
            device_id_type=MESH,
        )
        copy.start()
        sent.append(copy)
        return copy

    rows, width = trains.shape[1], slots.shape[2]
    depth, part_depth = train_ref.shape[2], query_ref.shape[1]
    half = rows // 2
    my_depth = pl.ds(pl.multiple_of(z * depth, depth), depth)
    my_part = pl.ds(pl.multiple_of(core * part_depth, part_depth), part_depth)

    own = [
        pltpu.make_async_copy(train_ref.at[z], trains.at[y, :, my_depth], own_sem.at[0]),
        pltpu.make_async_copy(query_ref, queries.at[x, z, :, my_part], own_sem.at[1]),
    ]
    for copy in own:
        copy.start()
    depth_of_stage = stage.shape[0]

    def fetch(source, index, place):
        return pltpu.make_async_copy(source.at[index], stage.at[place], stage_sem.at[place])

    for b in range(depth_of_stage):
        fetch(blocks_ref, b, b).start()

    barrier = pltpu.get_barrier_semaphore()
    for d in range(1, n_qry):
        there = turn(y, d // RING) * RING + turn(z, d % RING)
        pl.semaphore_signal(barrier, inc=1, device_id={"qry": there}, device_id_type=MESH)
    for d in range(1, n_ex):
        there = turn(x, d // 2) * 2 + (core + d % 2) % 2
        pl.semaphore_signal(barrier, inc=1, device_id={"ex": there}, device_id_type=MESH)
    pl.semaphore_wait(barrier, n_qry - 1 + n_ex - 1)

    def query_half(at_x, at_z, h):
        return queries.at[at_x, at_z, pl.ds(h * half, half), my_part]

    def query_sends(source, at_z):
        out = {}
        for h in range(2):
            for d in (1, 3):
                out[d, h] = send(source(h), query_half(x, at_z, h), dx=d)
        return out

    near_z = {}
    for h in range(2):
        for d in (1, 3):
            near_z[d, h] = send(query_ref.at[pl.ds(h * half, half)], query_half(x, z, h), dz=d)
    along_x = {0: query_sends(lambda h: query_ref.at[pl.ds(h * half, half)], z)}
    train_z = [
        send(train_ref.at[turn(z, d)], trains.at[y, :, my_depth], dz=d) for d in (1, 3, 2)
    ]

    held = coded.shape[0]
    pairs = parts.shape[1]

    def wanted(q, p):
        return cand_ref[q * (pairs // CANDS) + p // CANDS, p % CANDS]

    @pl.loop(0, n_qry)
    def _(q):
        block = jnp.int32(0)
        for p in range(pairs):
            item = wanted(q, p)
            block += jnp.where(item // held == qry, item % held, 0)
        pick[q] = block

    def code(b):
        place = b % depth_of_stage
        fetch(blocks_ref, b, place).wait()
        whole = stage[place]
        top = jnp.maximum(jnp.max(jnp.abs(whole), axis=1, keepdims=True), 1e-30)
        coded[b] = jnp.round(whole * (TOP / top)).astype(jnp.int32).astype(jnp.int16)
        wide = jnp.broadcast_to(top * (1.0 / TOP), (BLOCK_ROWS, BLOCK_ROWS))
        coded_scale[b] = jnp.transpose(wide)[:8]

    @pl.loop(0, depth_of_stage)
    def _(b):
        code(b)
        fetch(blocks_ref, b + depth_of_stage, b).start()

    @pl.loop(depth_of_stage, held)
    def _(b):
        code(b)
        fetch(tiles_ref, b - depth_of_stage, b - depth_of_stage).start()

    @pl.loop(0, n_qry)
    def _(q):
        leaving[q] = coded[pick[q]]
        leaving_scale[q] = coded_scale[pick[q]]

    slots[qry] = coded[pick[qry]]
    slot_scale[qry] = coded_scale[pick[qry]]

    slot_copies = []
    order = ((0, 1), (1, 0), (0, 3), (3, 0), (1, 1), (3, 3), (1, 3), (3, 1), (2, 1), (1, 2), (2, 3), (3, 2), (0, 2), (2, 0), (2, 2))
    chunk = BLOCK_ROWS // SLOT_CHUNKS

    def slot_round(r):
        for dy, dz in order:
            there = turn(y, dy) * RING + turn(z, dz)
            if r == 0:
                slot_copies.append(send(leaving_scale.at[there], slot_scale.at[qry], dy=dy, dz=dz))
            part = pl.ds(r * chunk, chunk)
            slot_copies.append(send(leaving.at[there, part], slots.at[qry, part], dy=dy, dz=dz))

    slot_round(0)

    near_z[1, 0].wait_recv()
    far_z = {0: send(query_half(x, turn(z, 3), 0), query_half(x, turn(z, 3), 0), dz=1)}
    near_z[3, 1].wait_recv()
    far_z[1] = send(query_half(x, turn(z, 1), 1), query_half(x, turn(z, 1), 1), dz=3)
    near_z[1, 1].wait_recv()
    along_x[3] = query_sends(lambda h: query_half(x, turn(z, 3), h), turn(z, 3))
    near_z[3, 0].wait_recv()
    along_x[1] = query_sends(lambda h: query_half(x, turn(z, 1), h), turn(z, 1))

    for copy in train_z:
        copy.wait_recv()
    own[0].wait()

    def train_half(at_y, h):
        return trains.at[at_y, pl.ds(h * half, half)]

    near_y = {}
    for h in range(2):
        for d in (1, 3):
            near_y[d, h] = send(train_half(y, h), train_half(y, h), dy=d)
    slot_round(1)

    def relay_x(d):
        at_z = turn(z, d)
        along_x[d][1, 0].wait_recv()
        first = send(query_half(turn(x, 3), at_z, 0), query_half(turn(x, 3), at_z, 0), dx=1)
        along_x[d][3, 1].wait_recv()
        second = send(query_half(turn(x, 1), at_z, 1), query_half(turn(x, 1), at_z, 1), dx=3)
        return first, second

    far_x = {0: relay_x(0)}

    far_z[0].wait_recv()
    far_z[1].wait_recv()
    along_x[2] = query_sends(lambda h: query_half(x, turn(z, 2), h), turn(z, 2))
    near_y[1, 0].wait_recv()
    far_y = {0: send(train_half(turn(y, 3), 0), train_half(turn(y, 3), 0), dy=1)}
    near_y[3, 1].wait_recv()
    far_y[1] = send(train_half(turn(y, 1), 1), train_half(turn(y, 1), 1), dy=3)
    slot_round(2)

    @pl.loop(0, split.shape[1])
    def _(t):
        fetch(tiles_ref, t, t).wait()
        whole = stage[t]
        high = whole.astype(jnp.bfloat16)
        split[0, t] = high
        split[1, t] = (whole - high.astype(jnp.float32)).astype(jnp.bfloat16)

    own[1].wait()

    def complete(d):
        along_x[d][1, 1].wait_recv()
        along_x[d][3, 0].wait_recv()
        far_x[d][0].wait_recv()
        far_x[d][1].wait_recv()
        view = queries.at[:, turn(z, d), :, my_part]
        return send(view, view, dc=1)

    out_copies, stay = [], []

    def score(d, from_core):
        to = turn(z, d)
        from_core.wait_recv()

        @pl.loop(0, RING)
        def _(k):
            value = lax.dot_general(
                trains[k], queries[k, to], (((1,), (1,)), ((), ())), preferred_element_type=jnp.float32
            )

            @pl.when(k == 0)
            def _():
                product[...] = value

            @pl.when(k > 0)
            def _():
                product[...] += value

        value = product[...]
        top = jnp.maximum(jnp.max(jnp.abs(value), axis=1, keepdims=True), 1e-30)
        ready[d] = jnp.round(value * (TOP / top)).astype(jnp.int32).astype(jnp.int16)
        ready_scale[d] = jnp.transpose(jnp.broadcast_to(top * (1.0 / TOP), (rows, 128)))[:8]
        if d == 0:
            stay.append(pltpu.make_async_copy(ready.at[0], out_ref.at[z], own_sem.at[2]))
            stay.append(pltpu.make_async_copy(ready_scale.at[0], out_scale_ref.at[z], own_sem.at[3]))
            for copy in stay:
                copy.start()
            return
        out_copies.append(send(ready_scale.at[d], out_scale_ref.at[z], dz=d))
        for h in range(2):
            part = pl.ds(h * half, half)
            out_copies.append(send(ready.at[d, part], out_ref.at[z, part], dz=d))

    from_core = {0: complete(0)}
    far_x[3] = relay_x(3)
    slot_round(3)
    near_y[1, 1].wait_recv()
    near_y[3, 0].wait_recv()
    far_y[0].wait_recv()
    far_y[1].wait_recv()
    score(0, from_core[0])
    from_core[3] = complete(3)
    far_x[1] = relay_x(1)
    score(3, from_core[3])
    from_core[1] = complete(1)
    far_x[2] = relay_x(2)
    score(1, from_core[1])
    from_core[2] = complete(2)
    score(2, from_core[2])

    for copy in slot_copies:
        copy.wait_recv()
    step = 512

    @pl.loop(0, pairs)
    def _(p):
        slot = cand_ref[qry * (pairs // CANDS) + p // CANDS, p % CANDS] // held
        tile = p // CANDS
        total = jnp.zeros((BLOCK_ROWS, BLOCK_ROWS), jnp.float32)
        for c in range(0, width, step):
            block = slots[slot, :, c : c + step].astype(jnp.float32)
            high = block.astype(jnp.bfloat16)
            low = (block - high.astype(jnp.float32)).astype(jnp.bfloat16)
            tile_high, tile_low = split[0, tile, :, c : c + step], split[1, tile, :, c : c + step]
            for a, b in ((high, tile_high), (high, tile_low), (low, tile_high)):
                total += lax.dot_general(a, b, (((1,), (1,)), ((), ())), preferred_element_type=jnp.float32)
        tall = jnp.transpose(jnp.broadcast_to(slot_scale[slot][:1], (BLOCK_ROWS, BLOCK_ROWS)))
        parts[:, p] = (total * tall).reshape(parts.shape[0], parts.shape[2], BLOCK_ROWS)

    part_copies = []
    for d in range(1, n_ex):
        there = turn(x, d // 2) * 2 + (core + d % 2) % 2
        part_copies.append(send(parts.at[there], parts_in.at[d], dx=d // 2, dc=d % 2))
    total = parts[ex]
    for d, copy in enumerate(part_copies, 1):
        copy.wait_recv()
        total += parts_in[d]
    exact_ref[...] = total

    for copy in out_copies:
        copy.wait_recv()
    for copy in stay:
        copy.wait()
    for copy in sent:
        copy.wait_send()


def decode_kernel(codes_ref, scale_ref, weight_ref, scores_ref):
    line = scale_ref[0][:1] * weight_ref[0]
    tall = jnp.transpose(jnp.broadcast_to(line, (128, line.shape[1])))
    scores_ref[...] = codes_ref[0].astype(jnp.float32) * tall[:, :1]


def local(train_proj, query_proj, out_weight, train_feat, query_feat, candidates):
    n_qry, n_ex = lax.axis_size("qry"), lax.axis_size("ex")
    width = train_feat.shape[1]
    held_blocks = train_feat.shape[0] // BLOCK_ROWS
    tiles_here = query_feat.shape[0] // BLOCK_ROWS
    pairs = tiles_here * CANDS
    depth = train_proj.shape[1]
    rows = train_proj.shape[0] // RING
    columns, part_depth = query_proj.shape
    share = BLOCK_ROWS // n_ex
    any_space, vmem = pl.BlockSpec(memory_space=pl.ANY), pl.BlockSpec(memory_space=pltpu.VMEM)
    dma = pltpu.SemaphoreType.DMA
    result, result_scale, exact = pl.pallas_call(
        main_kernel,
        out_shape=[
            jax.ShapeDtypeStruct((RING, rows, columns), jnp.int16),
            jax.ShapeDtypeStruct((RING, 8, rows), jnp.float32),
            jax.ShapeDtypeStruct((pairs, share, BLOCK_ROWS), jnp.float32),
        ],
        in_specs=[pl.BlockSpec(memory_space=pltpu.SMEM)] + [any_space] * 4,
        out_specs=[any_space, any_space, vmem],
        scratch_shapes=[
            pltpu.SMEM((n_qry,), jnp.int32),
            pltpu.VMEM((tiles_here, BLOCK_ROWS, width), jnp.float32),
            pltpu.VMEM((held_blocks, BLOCK_ROWS, width), jnp.int16),
            pltpu.VMEM((held_blocks, 8, BLOCK_ROWS), jnp.float32),
            pltpu.VMEM((n_qry, BLOCK_ROWS, width), jnp.int16),
            pltpu.VMEM((n_qry, 8, BLOCK_ROWS), jnp.float32),
            pltpu.VMEM((RING, rows, RING * depth), jnp.bfloat16),
            pltpu.VMEM((RING, RING, columns, 2 * part_depth), jnp.bfloat16),
            pltpu.VMEM((n_qry, BLOCK_ROWS, width), jnp.int16),
            pltpu.VMEM((n_qry, 8, BLOCK_ROWS), jnp.float32),
            pltpu.VMEM((2, tiles_here, BLOCK_ROWS, width), jnp.bfloat16),
            pltpu.VMEM((rows, columns), jnp.float32),
            pltpu.VMEM((RING, rows, columns), jnp.int16),
            pltpu.VMEM((RING, 8, rows), jnp.float32),
            pltpu.VMEM((n_ex, pairs, share, BLOCK_ROWS), jnp.float32),
            pltpu.VMEM((n_ex, pairs, share, BLOCK_ROWS), jnp.float32),
            dma((tiles_here,)),
            dma((4,)),
            dma((COPIES,)),
            dma((COPIES,)),
        ],
        compiler_params=pltpu.CompilerParams(
            collective_id=0, has_side_effects=True, vmem_limit_bytes=61 * MIB
        ),
        name="main",
    )(
        candidates,
        train_proj.reshape(RING, rows, depth),
        query_proj,
        train_feat.reshape(held_blocks, BLOCK_ROWS, width),
        query_feat.reshape(tiles_here, BLOCK_ROWS, width),
    )
    scores = pl.pallas_call(
        decode_kernel,
        grid=(RING,),
        in_specs=[
            pl.BlockSpec((1, rows, columns), lambda i: (i, 0, 0)),
            pl.BlockSpec((1, 8, rows), lambda i: (i, 0, 0)),
            pl.BlockSpec((1, 1, rows), lambda i: (i, 0, 0)),
        ],
        out_specs=pl.BlockSpec((rows, columns), lambda i: (i, 0)),
        out_shape=jax.ShapeDtypeStruct((RING * rows, columns), jnp.float32),
        compiler_params=pltpu.CompilerParams(vmem_limit_bytes=24 * MIB),
        name="decode",
    )(result, result_scale, out_weight.reshape(RING, 1, rows))
    return scores, exact.reshape(tiles_here, CANDS, share, BLOCK_ROWS)


def solution(mesh):
    placed = (P("ex", "qry"), P("qry", "ex"), P("ex"), P("qry", "ex"), P("qry", "ex"), P())
    return jax.shard_map(
        local,
        mesh=mesh,
        in_specs=placed,
        out_specs=(P("ex", "qry"), P("qry", None, "ex", None)),
        check_vma=False,
    )
```

```python
import jax
import jax.numpy as jnp
from jax import lax
from jax.experimental import pallas as pl
from jax.experimental.pallas import tpu as pltpu
from jax.sharding import PartitionSpec as P

BLOCK_ROWS = 128
CANDS = 2
RING = 4
SLOT_CHUNKS = 2
COPIES = 136
TOP = 32752.0
MESH = pl.DeviceIdType.MESH
MIB = 1 << 20


def main_kernel(
    cand_ref, train_ref, query_ref, blocks_ref, tiles_ref,
    out_ref, out_scale_ref, exact_ref,
    pick, pair_block, pair_tile, stage, coded, coded_scale, tile0, tile1, tile2, tile3, tile_scale,
    block_scales, tile_scales, leaving, slots, trains, queries, product, ready, ready_scale,
    parts, parts_in, back, back_in,
    stage_sem, own_sem, send_sem, recv_sem,
):
    ex, qry = lax.axis_index("ex"), lax.axis_index("qry")
    n_ex, n_qry = parts.shape[1], RING * RING
    x, core, y, z = ex // 2, ex % 2, qry // RING, qry % RING
    turn = lambda a, d: (a + d) % RING
    sent = []

    def send(src, dst, dx=0, dc=0, dy=0, dz=0):
        there = {"ex": turn(x, dx) * 2 + (core + dc) % 2, "qry": turn(y, dy) * RING + turn(z, dz)}
        k = len(sent)
        copy = pltpu.make_async_remote_copy(
            src_ref=src,
            dst_ref=dst,
            send_sem=send_sem.at[k],
            recv_sem=recv_sem.at[k],
            device_id=there,
            device_id_type=MESH,
        )
        copy.start()
        sent.append(copy)
        return copy

    rows, width = trains.shape[1], slots.shape[3]
    depth, part_depth = train_ref.shape[2], query_ref.shape[1]
    half = rows // 2
    my_depth = pl.ds(pl.multiple_of(z * depth, depth), depth)
    my_part = pl.ds(pl.multiple_of(core * part_depth, part_depth), part_depth)

    own = [
        pltpu.make_async_copy(train_ref.at[z], trains.at[y, :, my_depth], own_sem.at[0]),
        pltpu.make_async_copy(query_ref, queries.at[x, z, :, my_part], own_sem.at[1]),
    ]
    for copy in own:
        copy.start()
    depth_of_stage = stage.shape[0]

    def fetch(source, index, place):
        return pltpu.make_async_copy(source.at[index], stage.at[place], stage_sem.at[place])

    for b in range(depth_of_stage):
        fetch(blocks_ref, b, b).start()

    barrier = pltpu.get_barrier_semaphore()
    for d in range(1, n_qry):
        there = turn(y, d // RING) * RING + turn(z, d % RING)
        pl.semaphore_signal(barrier, inc=1, device_id={"qry": there}, device_id_type=MESH)
    for d in range(1, n_ex):
        there = turn(x, d // 2) * 2 + (core + d % 2) % 2
        pl.semaphore_signal(barrier, inc=1, device_id={"ex": there}, device_id_type=MESH)
    pl.semaphore_wait(barrier, n_qry - 1 + n_ex - 1)

    def query_half(at_x, at_z, h):
        return queries.at[at_x, at_z, pl.ds(h * half, half), my_part]

    def query_sends(source, at_z):
        out = {}
        for h in range(2):
            for d in (1, 3):
                out[d, h] = send(source(h), query_half(x, at_z, h), dx=d)
        return out

    near_z = {}
    for h in range(2):
        for d in (1, 3):
            near_z[d, h] = send(query_ref.at[pl.ds(h * half, half)], query_half(x, z, h), dz=d)
    along_x = {0: query_sends(lambda h: query_ref.at[pl.ds(h * half, half)], z)}
    train_z = [
        send(train_ref.at[turn(z, d)], trains.at[y, :, my_depth], dz=d) for d in (1, 3, 2)
    ]

    held, n_tiles = coded.shape[0], tile0.shape[0]
    pairs = n_tiles * CANDS

    def wanted(q, p):
        return cand_ref[q * n_tiles + p // CANDS, p % CANDS]

    @pl.loop(0, n_qry)
    def _(i):
        row, ring = i % RING, turn(z, i // RING)
        here, block, tile = jnp.int32(0), jnp.int32(0), jnp.int32(0)
        for p in range(pairs):
            place = wanted(row * RING + ring, p) - qry * held
            here = jnp.where((place >= 0) & (place < held), place, here)
            place = wanted(y * RING + ring, p) - (row * RING + z) * held
            match = (place >= 0) & (place < held)
            block = jnp.where(match, place, block)
            tile = jnp.where(match, p // CANDS, tile)
        pick[i] = here
        pair_block[i] = block
        pair_tile[i] = tile

    def code(place, to, at, line_to):
        whole = stage[place]
        top = jnp.maximum(jnp.max(jnp.abs(whole), axis=1, keepdims=True), 1e-30)
        to[at] = jnp.round(whole * (TOP / top)).astype(jnp.int32).astype(jnp.int16)
        wide = jnp.broadcast_to(top * (1.0 / TOP), (BLOCK_ROWS, BLOCK_ROWS))
        line_to[pl.ds(at, 1)] = jnp.transpose(wide)[:1].reshape(1, 1, BLOCK_ROWS)

    for b in range(held):
        place = b % depth_of_stage
        fetch(blocks_ref, b, place).wait()
        code(place, coded, b, coded_scale)
        if b + depth_of_stage < held:
            fetch(blocks_ref, b + depth_of_stage, place).start()
        else:
            fetch(tiles_ref, b + depth_of_stage - held, place).start()

    block_scales[y] = coded_scale[...]
    slot_copies = {d: [] for d in range(RING)}
    for d in range(1, RING):
        slot_copies[0].append(send(coded_scale, block_scales.at[y], dy=d))
    chunk = BLOCK_ROWS // SLOT_CHUNKS

    def slot_group(d):
        slots[y, d] = coded[pick[d * RING + y]]
        for dy in range(1, RING):
            leaving[dy - 1, d] = coded[pick[d * RING + turn(y, dy)]]
        for r in range(SLOT_CHUNKS):
            part = pl.ds(r * chunk, chunk)
            for dy in (1, 3, 2):
                slot_copies[d].append(send(leaving.at[dy - 1, d, part], slots.at[y, d, part], dy=dy))

    slot_group(0)

    tile_at = [tile0, tile1, tile2, tile3]
    for t in range(n_tiles):
        fetch(tiles_ref, t, t).wait()
        code(t, tile0, t, tile_scale)
    tile_scales[0] = tile_scale[...]
    scale_copies = [send(tile_scale, tile_scales.at[RING - d], dz=d) for d in range(1, RING)]

    near_tile = {}
    for k in range(n_tiles):
        near_tile[1, k] = send(tile0.at[k], tile3.at[k], dz=1)
        k = n_tiles - 1 - k
        near_tile[3, k] = send(tile0.at[k], tile1.at[k], dz=3)

    near_z[1, 0].wait_recv()
    far_z = {0: send(query_half(x, turn(z, 3), 0), query_half(x, turn(z, 3), 0), dz=1)}
    near_z[3, 1].wait_recv()
    far_z[1] = send(query_half(x, turn(z, 1), 1), query_half(x, turn(z, 1), 1), dz=3)
    near_z[1, 1].wait_recv()
    along_x[3] = query_sends(lambda h: query_half(x, turn(z, 3), h), turn(z, 3))
    near_z[3, 0].wait_recv()
    along_x[1] = query_sends(lambda h: query_half(x, turn(z, 1), h), turn(z, 1))

    for copy in train_z:
        copy.wait_recv()
    own[0].wait()

    def train_half(at_y, h):
        return trains.at[at_y, pl.ds(h * half, half)]

    near_y = {}
    for h in range(2):
        for d in (1, 3):
            near_y[d, h] = send(train_half(y, h), train_half(y, h), dy=d)
    slot_group(3)

    def relay_x(d):
        at_z = turn(z, d)
        along_x[d][1, 0].wait_recv()
        first = send(query_half(turn(x, 3), at_z, 0), query_half(turn(x, 3), at_z, 0), dx=1)
        along_x[d][3, 1].wait_recv()
        second = send(query_half(turn(x, 1), at_z, 1), query_half(turn(x, 1), at_z, 1), dx=3)
        return first, second

    far_x = {0: relay_x(0)}

    far_z[0].wait_recv()
    far_z[1].wait_recv()
    along_x[2] = query_sends(lambda h: query_half(x, turn(z, 2), h), turn(z, 2))
    near_y[1, 0].wait_recv()
    far_y = {0: send(train_half(turn(y, 3), 0), train_half(turn(y, 3), 0), dy=1)}
    near_y[3, 1].wait_recv()
    far_y[1] = send(train_half(turn(y, 1), 1), train_half(turn(y, 1), 1), dy=3)
    slot_group(1)

    far_tile = []
    for k in range(n_tiles // 2):
        near_tile[1, k].wait_recv()
        far_tile.append(send(tile3.at[k], tile2.at[k], dz=1))
        k = n_tiles - 1 - k
        near_tile[3, k].wait_recv()
        far_tile.append(send(tile1.at[k], tile2.at[k], dz=3))
    slot_group(2)

    own[1].wait()

    def complete(d):
        along_x[d][1, 1].wait_recv()
        along_x[d][3, 0].wait_recv()
        far_x[d][0].wait_recv()
        far_x[d][1].wait_recv()
        view = queries.at[:, turn(z, d), :, my_part]
        return send(view, view, dc=1)

    out_copies, stay = [], []

    def score(d, from_core):
        to = turn(z, d)
        from_core.wait_recv()

        @pl.loop(0, RING)
        def _(k):
            value = lax.dot_general(
                trains[k], queries[k, to], (((1,), (1,)), ((), ())), preferred_element_type=jnp.float32
            )

            @pl.when(k == 0)
            def _():
                product[...] = value

            @pl.when(k > 0)
            def _():
                product[...] += value

        value = product[...]
        top = jnp.maximum(jnp.max(jnp.abs(value), axis=1, keepdims=True), 1e-30)
        ready[d] = jnp.round(value * (TOP / top)).astype(jnp.int32).astype(jnp.int16)
        ready_scale[d] = jnp.transpose(jnp.broadcast_to(top * (1.0 / TOP), (rows, 128)))[:8]
        if d == 0:
            stay.append(pltpu.make_async_copy(ready.at[0], out_ref.at[z], own_sem.at[2]))
            stay.append(pltpu.make_async_copy(ready_scale.at[0], out_scale_ref.at[z], own_sem.at[3]))
            for copy in stay:
                copy.start()
            return
        out_copies.append(send(ready_scale.at[d], out_scale_ref.at[z], dz=d))
        for h in range(2):
            part = pl.ds(h * half, half)
            out_copies.append(send(ready.at[d, part], out_ref.at[z, part], dz=d))

    step = 512

    def halves(codes):
        value = codes.astype(jnp.float32)
        high = value.astype(jnp.bfloat16)
        return high, (value - high.astype(jnp.float32)).astype(jnp.bfloat16)

    def line_of(lines, index):
        row = lax.broadcasted_iota(jnp.int32, lines.shape, 0)
        return jnp.sum(jnp.where(row == index, lines, 0.0), axis=0, keepdims=True)

    part_copies, back_copies = {}, []

    def exact_dots(d):
        if d in (1, 3):
            for k in range(n_tiles // 2):
                k = k if d == 1 else n_tiles - 1 - k
                near_tile[RING - d, k].wait_recv()
        if d == 2:
            for copy in far_tile:
                copy.wait_recv()
        for copy in slot_copies[d]:
            copy.wait_recv()

        @pl.loop(0, RING)
        def _(j):
            block, tile = pair_block[d * RING + j], pair_tile[d * RING + j]
            total = jnp.zeros((BLOCK_ROWS, BLOCK_ROWS), jnp.float32)
            for c in range(0, width, step):
                high, low = halves(slots[j, d, :, c : c + step])
                tile_high, tile_low = halves(tile_at[d][tile, :, c : c + step])
                for a, b in ((high, tile_high), (high, tile_low), (low, tile_high)):
                    total += lax.dot_general(a, b, (((1,), (1,)), ((), ())), preferred_element_type=jnp.float32)
            line = line_of(block_scales[j, :, 0], block)
            tall = jnp.transpose(jnp.broadcast_to(line, (BLOCK_ROWS, BLOCK_ROWS)))
            total = total * tall * line_of(tile_scales[d, :, 0], tile)
            parts[d, :, j] = total.reshape(n_ex, parts.shape[3], BLOCK_ROWS)

        part_copies[d] = []
        for k in range(1, n_ex):
            there = turn(x, k // 2) * 2 + (core + k % 2) % 2
            part_copies[d].append(send(parts.at[d, there], parts_in.at[d, k], dx=k // 2, dc=k % 2))

    def exact_sum(d):
        total = parts[d, ex]
        for k, copy in enumerate(part_copies[d], 1):
            copy.wait_recv()
            total += parts_in[d, k]
        if d == 0:
            back_in[z] = total
        else:
            back[d] = total
            back_copies.append(send(back.at[d], back_in.at[z], dz=d))

    from_core = {0: complete(0)}
    far_x[3] = relay_x(3)
    near_y[1, 1].wait_recv()
    near_y[3, 0].wait_recv()
    far_y[0].wait_recv()
    far_y[1].wait_recv()
    score(0, from_core[0])
    for copy in scale_copies:
        copy.wait_recv()
    exact_dots(0)
    from_core[3] = complete(3)
    far_x[1] = relay_x(1)
    score(3, from_core[3])
    from_core[1] = complete(1)
    far_x[2] = relay_x(2)
    score(1, from_core[1])
    from_core[2] = complete(2)
    score(2, from_core[2])
    exact_dots(3)
    exact_sum(0)
    exact_dots(1)
    exact_sum(3)
    exact_dots(2)

    exact_sum(1)
    exact_sum(2)
    for copy in back_copies:
        copy.wait_recv()
    for p in range(pairs):
        owner = wanted(qry, p) // held
        exact_ref[p] = back_in[owner % RING, owner // RING]

    for copy in out_copies:
        copy.wait_recv()
    for copy in stay:
        copy.wait()
    for copy in sent:
        copy.wait_send()


def decode_kernel(codes_ref, scale_ref, weight_ref, scores_ref):
    line = scale_ref[0][:1] * weight_ref[0]
    tall = jnp.transpose(jnp.broadcast_to(line, (128, line.shape[1])))
    scores_ref[...] = codes_ref[0].astype(jnp.float32) * tall[:, :1]


def local(train_proj, query_proj, out_weight, train_feat, query_feat, candidates):
    n_qry, n_ex = lax.axis_size("qry"), lax.axis_size("ex")
    width = train_feat.shape[1]
    held_blocks = train_feat.shape[0] // BLOCK_ROWS
    tiles_here = query_feat.shape[0] // BLOCK_ROWS
    pairs = tiles_here * CANDS
    depth = train_proj.shape[1]
    rows = train_proj.shape[0] // RING
    columns, part_depth = query_proj.shape
    share = BLOCK_ROWS // n_ex
    any_space, vmem = pl.BlockSpec(memory_space=pl.ANY), pl.BlockSpec(memory_space=pltpu.VMEM)
    dma = pltpu.SemaphoreType.DMA
    result, result_scale, exact = pl.pallas_call(
        main_kernel,
        out_shape=[
            jax.ShapeDtypeStruct((RING, rows, columns), jnp.int16),
            jax.ShapeDtypeStruct((RING, 8, rows), jnp.float32),
            jax.ShapeDtypeStruct((pairs, share, BLOCK_ROWS), jnp.float32),
        ],
        in_specs=[pl.BlockSpec(memory_space=pltpu.SMEM)] + [any_space] * 4,
        out_specs=[any_space, any_space, vmem],
        scratch_shapes=[
            pltpu.SMEM((n_qry,), jnp.int32),
            pltpu.SMEM((n_qry,), jnp.int32),
            pltpu.SMEM((n_qry,), jnp.int32),
            pltpu.VMEM((tiles_here, BLOCK_ROWS, width), jnp.float32),
            pltpu.VMEM((held_blocks, BLOCK_ROWS, width), jnp.int16),
            pltpu.VMEM((held_blocks, 1, BLOCK_ROWS), jnp.float32),
            pltpu.VMEM((tiles_here, BLOCK_ROWS, width), jnp.int16),
            pltpu.VMEM((tiles_here, BLOCK_ROWS, width), jnp.int16),
            pltpu.VMEM((tiles_here, BLOCK_ROWS, width), jnp.int16),
            pltpu.VMEM((tiles_here, BLOCK_ROWS, width), jnp.int16),
            pltpu.VMEM((tiles_here, 1, BLOCK_ROWS), jnp.float32),
            pltpu.VMEM((RING, held_blocks, 1, BLOCK_ROWS), jnp.float32),
            pltpu.VMEM((RING, tiles_here, 1, BLOCK_ROWS), jnp.float32),
            pltpu.VMEM((RING - 1, RING, BLOCK_ROWS, width), jnp.int16),
            pltpu.VMEM((RING, RING, BLOCK_ROWS, width), jnp.int16),
            pltpu.VMEM((RING, rows, RING * depth), jnp.bfloat16),
            pltpu.VMEM((RING, RING, columns, 2 * part_depth), jnp.bfloat16),
            pltpu.VMEM((rows, columns), jnp.float32),
            pltpu.VMEM((RING, rows, columns), jnp.int16),
            pltpu.VMEM((RING, 8, rows), jnp.float32),
            pltpu.VMEM((RING, n_ex, RING, share, BLOCK_ROWS), jnp.float32),
            pltpu.VMEM((RING, n_ex, RING, share, BLOCK_ROWS), jnp.float32),
            pltpu.VMEM((RING, RING, share, BLOCK_ROWS), jnp.float32),
            pltpu.VMEM((RING, RING, share, BLOCK_ROWS), jnp.float32),
            dma((tiles_here,)),
            dma((4,)),
            dma((COPIES,)),
            dma((COPIES,)),
        ],
        compiler_params=pltpu.CompilerParams(
            collective_id=0, has_side_effects=True, vmem_limit_bytes=61 * MIB
        ),
        name="main",
    )(
        candidates,
        train_proj.reshape(RING, rows, depth),
        query_proj,
        train_feat.reshape(held_blocks, BLOCK_ROWS, width),
        query_feat.reshape(tiles_here, BLOCK_ROWS, width),
    )
    scores = pl.pallas_call(
        decode_kernel,
        grid=(RING,),
        in_specs=[
            pl.BlockSpec((1, rows, columns), lambda i: (i, 0, 0)),
            pl.BlockSpec((1, 8, rows), lambda i: (i, 0, 0)),
            pl.BlockSpec((1, 1, rows), lambda i: (i, 0, 0)),
        ],
        out_specs=pl.BlockSpec((rows, columns), lambda i: (i, 0)),
        out_shape=jax.ShapeDtypeStruct((RING * rows, columns), jnp.float32),
        compiler_params=pltpu.CompilerParams(vmem_limit_bytes=24 * MIB),
        name="decode",
    )(result, result_scale, out_weight.reshape(RING, 1, rows))
    return scores, exact.reshape(tiles_here, CANDS, share, BLOCK_ROWS)


def solution(mesh):
    placed = (P("ex", "qry"), P("qry", "ex"), P("ex"), P("qry", "ex"), P("qry", "ex"), P())
    return jax.shard_map(
        local,
        mesh=mesh,
        in_specs=placed,
        out_specs=(P("ex", "qry"), P("qry", None, "ex", None)),
        check_vma=False,
    )
```

```python
import jax
import jax.numpy as jnp
from jax import lax
from jax.experimental import pallas as pl
from jax.experimental.pallas import tpu as pltpu
from jax.sharding import PartitionSpec as P

BLOCK_ROWS = 128
CANDS = 2
RING = 4
SLOT_CHUNKS = 2
COPIES = 136
TOP = 32752.0
MESH = pl.DeviceIdType.MESH
MIB = 1 << 20


def main_kernel(
    cand_ref, train_ref, query_ref, blocks_ref, tiles_ref,
    out_ref, out_scale_ref, exact_ref,
    pick, pair_block, pair_tile, stage, coded, coded_scale, tile0, tile1, tile2, tile3, tile_scale,
    block_scales, tile_scales, leaving, slots, trains, queries, product, ready, ready_scale,
    parts, parts_in, back, back_in,
    stage_sem, own_sem, send_sem, recv_sem,
):
    ex, qry = lax.axis_index("ex"), lax.axis_index("qry")
    n_ex, n_qry = parts.shape[1], RING * RING
    x, core, y, z = ex // 2, ex % 2, qry // RING, qry % RING
    turn = lambda a, d: (a + d) % RING
    sent = []

    def send(src, dst, dx=0, dc=0, dy=0, dz=0):
        there = {"ex": turn(x, dx) * 2 + (core + dc) % 2, "qry": turn(y, dy) * RING + turn(z, dz)}
        k = len(sent)
        copy = pltpu.make_async_remote_copy(
            src_ref=src,
            dst_ref=dst,
            send_sem=send_sem.at[k],
            recv_sem=recv_sem.at[k],
            device_id=there,
            device_id_type=MESH,
        )
        copy.start()
        sent.append(copy)
        return copy

    rows, width = trains.shape[1], slots.shape[3]
    depth, part_depth = train_ref.shape[2], query_ref.shape[1]
    half = rows // 2
    my_depth = pl.ds(pl.multiple_of(z * depth, depth), depth)
    my_part = pl.ds(pl.multiple_of(core * part_depth, part_depth), part_depth)

    own = [
        pltpu.make_async_copy(train_ref.at[z], trains.at[y, :, my_depth], own_sem.at[0]),
        pltpu.make_async_copy(query_ref, queries.at[x, z, :, my_part], own_sem.at[1]),
    ]
    for copy in own:
        copy.start()
    depth_of_stage = stage.shape[0]

    def fetch(source, index, place):
        return pltpu.make_async_copy(source.at[index], stage.at[place], stage_sem.at[place])

    for b in range(depth_of_stage):
        fetch(blocks_ref, b, b).start()

    barrier = pltpu.get_barrier_semaphore()
    for d in range(1, n_qry):
        there = turn(y, d // RING) * RING + turn(z, d % RING)
        pl.semaphore_signal(barrier, inc=1, device_id={"qry": there}, device_id_type=MESH)
    for d in range(1, n_ex):
        there = turn(x, d // 2) * 2 + (core + d % 2) % 2
        pl.semaphore_signal(barrier, inc=1, device_id={"ex": there}, device_id_type=MESH)
    pl.semaphore_wait(barrier, n_qry - 1 + n_ex - 1)

    def query_half(at_x, at_z, h):
        return queries.at[at_x, at_z, pl.ds(h * half, half), my_part]

    def query_sends(source, at_z):
        out = {}
        for h in range(2):
            for d in (1, 3):
                out[d, h] = send(source(h), query_half(x, at_z, h), dx=d)
        return out

    near_z = {}
    for h in range(2):
        for d in (1, 3):
            near_z[d, h] = send(query_ref.at[pl.ds(h * half, half)], query_half(x, z, h), dz=d)
    along_x = {0: query_sends(lambda h: query_ref.at[pl.ds(h * half, half)], z)}
    train_z = [
        send(train_ref.at[turn(z, d)], trains.at[y, :, my_depth], dz=d) for d in (1, 3, 2)
    ]

    near_y, far_y = {}, {}

    def train_part(at_y, d, first=0, many=None):
        columns = pl.ds(pl.multiple_of(turn(z, d) * depth, depth), depth)
        return trains.at[at_y, pl.ds(first, many or rows), columns]

    def train_sends(d, source):
        for dy in (1, 3):
            near_y[d, dy] = send(source, train_part(y, d), dy=dy)

    def train_relay(d):
        for dy, first in ((1, 0), (3, half)):
            near_y[d, dy].wait_recv()
            view = train_part(turn(y, RING - dy), d, first, half)
            far_y[d, dy] = send(view, view, dy=dy)

    train_sends(0, train_ref.at[z])

    held, n_tiles = coded.shape[0], tile0.shape[0]
    pairs = n_tiles * CANDS

    def wanted(q, p):
        return cand_ref[q * n_tiles + p // CANDS, p % CANDS]

    @pl.loop(0, n_qry)
    def _(i):
        row, ring = i % RING, turn(z, i // RING)
        here, block, tile = jnp.int32(0), jnp.int32(0), jnp.int32(0)
        for p in range(pairs):
            place = wanted(row * RING + ring, p) - qry * held
            here = jnp.where((place >= 0) & (place < held), place, here)
            place = wanted(y * RING + ring, p) - (row * RING + z) * held
            match = (place >= 0) & (place < held)
            block = jnp.where(match, place, block)
            tile = jnp.where(match, p // CANDS, tile)
        pick[i] = here
        pair_block[i] = block
        pair_tile[i] = tile

    def code(place, to, at, line_to):
        whole = stage[place]
        top = jnp.maximum(jnp.max(jnp.abs(whole), axis=1, keepdims=True), 1e-30)
        to[at] = jnp.round(whole * (TOP / top)).astype(jnp.int32).astype(jnp.int16)
        wide = jnp.broadcast_to(top * (1.0 / TOP), (BLOCK_ROWS, BLOCK_ROWS))
        line_to[pl.ds(at, 1)] = jnp.transpose(wide)[:1].reshape(1, 1, BLOCK_ROWS)

    for b in range(held):
        place = b % depth_of_stage
        fetch(blocks_ref, b, place).wait()
        code(place, coded, b, coded_scale)
        if b + depth_of_stage < held:
            fetch(blocks_ref, b + depth_of_stage, place).start()
        else:
            fetch(tiles_ref, b + depth_of_stage - held, place).start()

    block_scales[y] = coded_scale[...]
    slot_copies = {d: [] for d in range(RING)}
    for d in range(1, RING):
        slot_copies[0].append(send(coded_scale, block_scales.at[y], dy=d))
    chunk = BLOCK_ROWS // SLOT_CHUNKS

    def slot_group(d):
        slots[y, d] = coded[pick[d * RING + y]]
        for dy in range(1, RING):
            leaving[dy - 1, d] = coded[pick[d * RING + turn(y, dy)]]
        for r in range(SLOT_CHUNKS):
            part = pl.ds(r * chunk, chunk)
            for dy in (1, 3, 2):
                slot_copies[d].append(send(leaving.at[dy - 1, d, part], slots.at[y, d, part], dy=dy))

    slot_group(0)

    tile_at = [tile0, tile1, tile2, tile3]
    for t in range(n_tiles):
        fetch(tiles_ref, t, t).wait()
        code(t, tile0, t, tile_scale)
    tile_scales[0] = tile_scale[...]
    scale_copies = [send(tile_scale, tile_scales.at[RING - d], dz=d) for d in range(1, RING)]

    near_z[1, 0].wait_recv()
    far_z = {0: send(query_half(x, turn(z, 3), 0), query_half(x, turn(z, 3), 0), dz=1)}
    near_z[3, 1].wait_recv()
    far_z[1] = send(query_half(x, turn(z, 1), 1), query_half(x, turn(z, 1), 1), dz=3)
    near_z[1, 1].wait_recv()
    along_x[3] = query_sends(lambda h: query_half(x, turn(z, 3), h), turn(z, 3))
    near_z[3, 0].wait_recv()
    along_x[1] = query_sends(lambda h: query_half(x, turn(z, 1), h), turn(z, 1))

    train_relay(0)
    for d, copy in zip((3, 1, 2), train_z):
        copy.wait_recv()
        train_sends(d, train_part(y, d))
    near_tile = {}
    for k in range(n_tiles):
        near_tile[1, k] = send(tile0.at[k], tile3.at[k], dz=1)
        k = n_tiles - 1 - k
        near_tile[3, k] = send(tile0.at[k], tile1.at[k], dz=3)

    slot_group(3)

    def relay_x(d):
        at_z = turn(z, d)
        along_x[d][1, 0].wait_recv()
        first = send(query_half(turn(x, 3), at_z, 0), query_half(turn(x, 3), at_z, 0), dx=1)
        along_x[d][3, 1].wait_recv()
        second = send(query_half(turn(x, 1), at_z, 1), query_half(turn(x, 1), at_z, 1), dx=3)
        return first, second

    far_x = {0: relay_x(0)}

    far_z[0].wait_recv()
    far_z[1].wait_recv()
    along_x[2] = query_sends(lambda h: query_half(x, turn(z, 2), h), turn(z, 2))
    for d in (3, 1, 2):
        train_relay(d)
    slot_group(1)

    far_tile = []
    for k in range(n_tiles // 2):
        near_tile[1, k].wait_recv()
        far_tile.append(send(tile3.at[k], tile2.at[k], dz=1))
        k = n_tiles - 1 - k
        near_tile[3, k].wait_recv()
        far_tile.append(send(tile1.at[k], tile2.at[k], dz=3))
    slot_group(2)

    own[1].wait()

    def complete(d):
        along_x[d][1, 1].wait_recv()
        along_x[d][3, 0].wait_recv()
        far_x[d][0].wait_recv()
        far_x[d][1].wait_recv()
        view = queries.at[:, turn(z, d), :, my_part]
        return send(view, view, dc=1)

    out_copies, stay = [], []

    def score(d, from_core):
        to = turn(z, d)
        from_core.wait_recv()

        @pl.loop(0, RING)
        def _(k):
            value = lax.dot_general(
                trains[k], queries[k, to], (((1,), (1,)), ((), ())), preferred_element_type=jnp.float32
            )

            @pl.when(k == 0)
            def _():
                product[...] = value

            @pl.when(k > 0)
            def _():
                product[...] += value

        value = product[...]
        top = jnp.maximum(jnp.max(jnp.abs(value), axis=1, keepdims=True), 1e-30)
        ready[d] = jnp.round(value * (TOP / top)).astype(jnp.int32).astype(jnp.int16)
        ready_scale[d] = jnp.transpose(jnp.broadcast_to(top * (1.0 / TOP), (rows, 128)))[:8]
        if d == 0:
            stay.append(pltpu.make_async_copy(ready.at[0], out_ref.at[z], own_sem.at[2]))
            stay.append(pltpu.make_async_copy(ready_scale.at[0], out_scale_ref.at[z], own_sem.at[3]))
            for copy in stay:
                copy.start()
            return
        out_copies.append(send(ready_scale.at[d], out_scale_ref.at[z], dz=d))
        for h in range(2):
            part = pl.ds(h * half, half)
            out_copies.append(send(ready.at[d, part], out_ref.at[z, part], dz=d))

    step = 512

    def halves(codes):
        value = codes.astype(jnp.float32)
        high = value.astype(jnp.bfloat16)
        return high, (value - high.astype(jnp.float32)).astype(jnp.bfloat16)

    def line_of(lines, index):
        row = lax.broadcasted_iota(jnp.int32, lines.shape, 0)
        return jnp.sum(jnp.where(row == index, lines, 0.0), axis=0, keepdims=True)

    part_copies, back_copies = {}, []

    def exact_dots(d):
        if d in (1, 3):
            for k in range(n_tiles // 2):
                k = k if d == 1 else n_tiles - 1 - k
                near_tile[RING - d, k].wait_recv()
        if d == 2:
            for copy in far_tile:
                copy.wait_recv()
        for copy in slot_copies[d]:
            copy.wait_recv()

        @pl.loop(0, RING)
        def _(j):
            block, tile = pair_block[d * RING + j], pair_tile[d * RING + j]
            total = jnp.zeros((BLOCK_ROWS, BLOCK_ROWS), jnp.float32)
            for c in range(0, width, step):
                high, low = halves(slots[j, d, :, c : c + step])
                tile_high, tile_low = halves(tile_at[d][tile, :, c : c + step])
                for a, b in ((high, tile_high), (high, tile_low), (low, tile_high)):
                    total += lax.dot_general(a, b, (((1,), (1,)), ((), ())), preferred_element_type=jnp.float32)
            line = line_of(block_scales[j, :, 0], block)
            tall = jnp.transpose(jnp.broadcast_to(line, (BLOCK_ROWS, BLOCK_ROWS)))
            total = total * tall * line_of(tile_scales[d, :, 0], tile)
            parts[d, :, j] = total.reshape(n_ex, parts.shape[3], BLOCK_ROWS)

        part_copies[d] = []
        for k in range(1, n_ex):
            there = turn(x, k // 2) * 2 + (core + k % 2) % 2
            part_copies[d].append(send(parts.at[d, there], parts_in.at[d, k], dx=k // 2, dc=k % 2))

    def exact_sum(d):
        total = parts[d, ex]
        for k, copy in enumerate(part_copies[d], 1):
            copy.wait_recv()
            total += parts_in[d, k]
        if d == 0:
            back_in[z] = total
        else:
            back[d] = total
            back_copies.append(send(back.at[d], back_in.at[z], dz=d))

    from_core = {0: complete(0)}
    far_x[3] = relay_x(3)
    own[0].wait()
    for copy in far_y.values():
        copy.wait_recv()
    score(0, from_core[0])
    for copy in scale_copies:
        copy.wait_recv()
    exact_dots(0)
    from_core[3] = complete(3)
    far_x[1] = relay_x(1)
    score(3, from_core[3])
    from_core[1] = complete(1)
    far_x[2] = relay_x(2)
    score(1, from_core[1])
    from_core[2] = complete(2)
    score(2, from_core[2])
    exact_dots(3)
    exact_sum(0)
    exact_dots(1)
    exact_sum(3)
    exact_sum(1)
    exact_dots(2)

    exact_sum(2)
    for copy in back_copies:
        copy.wait_recv()
    for p in range(pairs):
        owner = wanted(qry, p) // held
        exact_ref[p] = back_in[owner % RING, owner // RING]

    for copy in out_copies:
        copy.wait_recv()
    for copy in stay:
        copy.wait()
    for copy in sent:
        copy.wait_send()


def decode_kernel(codes_ref, scale_ref, weight_ref, scores_ref):
    line = scale_ref[0][:1] * weight_ref[0]
    tall = jnp.transpose(jnp.broadcast_to(line, (128, line.shape[1])))
    scores_ref[...] = codes_ref[0].astype(jnp.float32) * tall[:, :1]


def local(train_proj, query_proj, out_weight, train_feat, query_feat, candidates):
    n_qry, n_ex = lax.axis_size("qry"), lax.axis_size("ex")
    width = train_feat.shape[1]
    held_blocks = train_feat.shape[0] // BLOCK_ROWS
    tiles_here = query_feat.shape[0] // BLOCK_ROWS
    pairs = tiles_here * CANDS
    depth = train_proj.shape[1]
    rows = train_proj.shape[0] // RING
    columns, part_depth = query_proj.shape
    share = BLOCK_ROWS // n_ex
    any_space, vmem = pl.BlockSpec(memory_space=pl.ANY), pl.BlockSpec(memory_space=pltpu.VMEM)
    dma = pltpu.SemaphoreType.DMA
    result, result_scale, exact = pl.pallas_call(
        main_kernel,
        out_shape=[
            jax.ShapeDtypeStruct((RING, rows, columns), jnp.int16),
            jax.ShapeDtypeStruct((RING, 8, rows), jnp.float32),
            jax.ShapeDtypeStruct((pairs, share, BLOCK_ROWS), jnp.float32),
        ],
        in_specs=[pl.BlockSpec(memory_space=pltpu.SMEM)] + [any_space] * 4,
        out_specs=[any_space, any_space, vmem],
        scratch_shapes=[
            pltpu.SMEM((n_qry,), jnp.int32),
            pltpu.SMEM((n_qry,), jnp.int32),
            pltpu.SMEM((n_qry,), jnp.int32),
            pltpu.VMEM((tiles_here, BLOCK_ROWS, width), jnp.float32),
            pltpu.VMEM((held_blocks, BLOCK_ROWS, width), jnp.int16),
            pltpu.VMEM((held_blocks, 1, BLOCK_ROWS), jnp.float32),
            pltpu.VMEM((tiles_here, BLOCK_ROWS, width), jnp.int16),
            pltpu.VMEM((tiles_here, BLOCK_ROWS, width), jnp.int16),
            pltpu.VMEM((tiles_here, BLOCK_ROWS, width), jnp.int16),
            pltpu.VMEM((tiles_here, BLOCK_ROWS, width), jnp.int16),
            pltpu.VMEM((tiles_here, 1, BLOCK_ROWS), jnp.float32),
            pltpu.VMEM((RING, held_blocks, 1, BLOCK_ROWS), jnp.float32),
            pltpu.VMEM((RING, tiles_here, 1, BLOCK_ROWS), jnp.float32),
            pltpu.VMEM((RING - 1, RING, BLOCK_ROWS, width), jnp.int16),
            pltpu.VMEM((RING, RING, BLOCK_ROWS, width), jnp.int16),
            pltpu.VMEM((RING, rows, RING * depth), jnp.bfloat16),
            pltpu.VMEM((RING, RING, columns, 2 * part_depth), jnp.bfloat16),
            pltpu.VMEM((rows, columns), jnp.float32),
            pltpu.VMEM((RING, rows, columns), jnp.int16),
            pltpu.VMEM((RING, 8, rows), jnp.float32),
            pltpu.VMEM((RING, n_ex, RING, share, BLOCK_ROWS), jnp.float32),
            pltpu.VMEM((RING, n_ex, RING, share, BLOCK_ROWS), jnp.float32),
            pltpu.VMEM((RING, RING, share, BLOCK_ROWS), jnp.float32),
            pltpu.VMEM((RING, RING, share, BLOCK_ROWS), jnp.float32),
            dma((tiles_here,)),
            dma((4,)),
            dma((COPIES,)),
            dma((COPIES,)),
        ],
        compiler_params=pltpu.CompilerParams(
            collective_id=0, has_side_effects=True, vmem_limit_bytes=61 * MIB
        ),
        name="main",
    )(
        candidates,
        train_proj.reshape(RING, rows, depth),
        query_proj,
        train_feat.reshape(held_blocks, BLOCK_ROWS, width),
        query_feat.reshape(tiles_here, BLOCK_ROWS, width),
    )
    scores = pl.pallas_call(
        decode_kernel,
        grid=(RING,),
        in_specs=[
            pl.BlockSpec((1, rows, columns), lambda i: (i, 0, 0)),
            pl.BlockSpec((1, 8, rows), lambda i: (i, 0, 0)),
            pl.BlockSpec((1, 1, rows), lambda i: (i, 0, 0)),
        ],
        out_specs=pl.BlockSpec((rows, columns), lambda i: (i, 0)),
        out_shape=jax.ShapeDtypeStruct((RING * rows, columns), jnp.float32),
        compiler_params=pltpu.CompilerParams(vmem_limit_bytes=60 * MIB),
        name="decode",
    )(result, result_scale, out_weight.reshape(RING, 1, rows))
    return scores, exact.reshape(tiles_here, CANDS, share, BLOCK_ROWS)


def solution(mesh):
    placed = (P("ex", "qry"), P("qry", "ex"), P("ex"), P("qry", "ex"), P("qry", "ex"), P())
    return jax.shard_map(
        local,
        mesh=mesh,
        in_specs=placed,
        out_specs=(P("ex", "qry"), P("qry", None, "ex", None)),
        check_vma=False,
    )
```

```python
import jax
import jax.numpy as jnp
from jax import lax
from jax.experimental import pallas as pl
from jax.experimental.pallas import tpu as pltpu
from jax.sharding import PartitionSpec as P

BLOCK_ROWS = 128
CANDS = 2
RING = 4
SLOT_CHUNKS = 2
MEMBERS = 2
COPIES = 136
TOP = 32752.0
MESH = pl.DeviceIdType.MESH
MIB = 1 << 20


def main_kernel(
    cand_in_ref, train_ref, query_ref, blocks_ref, tiles_ref,
    out_ref, out_scale_ref, exact_ref,
    cand_ref, pick, pair_block, pair_tile, stage, coded, coded_scale, tile0, tile1, tile2, tile3, tile_scale,
    block_scales, tile_scales, leaving, slots, trains, queries, product, ready, ready_scale,
    parts, parts_in, back, back_in,
    stage_sem, own_sem, send_sem, recv_sem,
):
    ex, qry = lax.axis_index("ex"), lax.axis_index("qry")
    n_ex, n_qry = parts.shape[1], RING * RING
    x, core, y, z = ex // 2, ex % 2, qry // RING, qry % RING
    turn = lambda a, d: (a + d) % RING
    sent = []

    def send(src, dst, dx=0, dc=0, dy=0, dz=0):
        there = {"ex": turn(x, dx) * 2 + (core + dc) % 2, "qry": turn(y, dy) * RING + turn(z, dz)}
        k = len(sent)
        copy = pltpu.make_async_remote_copy(
            src_ref=src,
            dst_ref=dst,
            send_sem=send_sem.at[k],
            recv_sem=recv_sem.at[k],
            device_id=there,
            device_id_type=MESH,
        )
        copy.start()
        sent.append(copy)
        return copy

    rows, width = trains.shape[1], slots.shape[3]
    depth, part_depth = train_ref.shape[2], query_ref.shape[1]
    half = rows // 2
    my_depth = pl.ds(pl.multiple_of(z * depth, depth), depth)
    my_part = pl.ds(pl.multiple_of(core * part_depth, part_depth), part_depth)

    own = [
        pltpu.make_async_copy(train_ref.at[z], trains.at[y, :, my_depth], own_sem.at[0]),
        pltpu.make_async_copy(query_ref, queries.at[x, z, :, my_part], own_sem.at[1]),
    ]
    for copy in own:
        copy.start()
    cand_copy = pltpu.make_async_copy(cand_in_ref, cand_ref, own_sem.at[4])
    cand_copy.start()
    depth_of_stage = stage.shape[0]

    def fetch(source, index, place):
        return pltpu.make_async_copy(source.at[index], stage.at[place], stage_sem.at[place])

    for b in range(depth_of_stage):
        fetch(blocks_ref, b, b).start()

    barrier = pltpu.get_barrier_semaphore()
    for d in range(1, n_qry):
        there = turn(y, d // RING) * RING + turn(z, d % RING)
        pl.semaphore_signal(barrier, inc=1, device_id={"qry": there}, device_id_type=MESH)
    for d in range(1, n_ex):
        there = turn(x, d // 2) * 2 + (core + d % 2) % 2
        pl.semaphore_signal(barrier, inc=1, device_id={"ex": there}, device_id_type=MESH)
    pl.semaphore_wait(barrier, n_qry - 1 + n_ex - 1)

    def query_half(at_x, at_z, h):
        return queries.at[at_x, at_z, pl.ds(h * half, half), my_part]

    def query_sends(source, at_z):
        out = {}
        for h in range(2):
            for d in (1, 3):
                out[d, h] = send(source(h), query_half(x, at_z, h), dx=d)
        return out

    train_z = [
        send(train_ref.at[turn(z, d)], trains.at[y, :, my_depth], dz=d) for d in (1, 3, 2)
    ]

    near_z = {}
    for h in range(2):
        for d in (1, 3):
            near_z[d, h] = send(query_ref.at[pl.ds(h * half, half)], query_half(x, z, h), dz=d)
    along_x = {0: query_sends(lambda h: query_ref.at[pl.ds(h * half, half)], z)}
    near_y, far_y = {}, {}

    def train_part(at_y, d, first=0, many=None):
        columns = pl.ds(pl.multiple_of(turn(z, d) * depth, depth), depth)
        return trains.at[at_y, pl.ds(first, many or rows), columns]

    def train_sends(d, source):
        for dy in (1, 3):
            near_y[d, dy] = send(source, train_part(y, d), dy=dy)

    def train_relay(d):
        for dy, first in ((1, 0), (3, half)):
            near_y[d, dy].wait_recv()
            view = train_part(turn(y, RING - dy), d, first, half)
            far_y[d, dy] = send(view, view, dy=dy)

    train_sends(0, train_ref.at[z])

    held, n_tiles = coded.shape[0], tile0.shape[0]
    pairs = n_tiles * CANDS

    def wanted(q, p):
        return cand_ref[p % CANDS, q * n_tiles + p // CANDS]

    cand_copy.wait()

    @pl.loop(0, n_qry)
    def _(i):
        row, ring = i % RING, turn(z, i // RING)
        here, block, tile = jnp.int32(0), jnp.int32(0), jnp.int32(0)
        for p in range(pairs):
            place = wanted(row * RING + ring, p) - qry * held
            here = jnp.where((place >= 0) & (place < held), place, here)
            place = wanted(y * RING + ring, p) - (row * RING + z) * held
            match = (place >= 0) & (place < held)
            block = jnp.where(match, place, block)
            tile = jnp.where(match, p // CANDS, tile)
        pick[i] = here
        pair_block[i] = block
        pair_tile[i] = tile

    def code(place, to, at, line_to):
        whole = stage[place]
        top = jnp.maximum(jnp.max(jnp.abs(whole), axis=1, keepdims=True), 1e-30)
        to[at] = jnp.round(whole * (TOP / top)).astype(jnp.int32).astype(jnp.int16)
        wide = jnp.broadcast_to(top * (1.0 / TOP), (BLOCK_ROWS, BLOCK_ROWS))
        line_to[pl.ds(at, 1)] = jnp.transpose(wide)[:1].reshape(1, 1, BLOCK_ROWS)

    for b in range(held):
        place = b % depth_of_stage
        fetch(blocks_ref, b, place).wait()
        code(place, coded, b, coded_scale)
        if b + depth_of_stage < held:
            fetch(blocks_ref, b + depth_of_stage, place).start()
        else:
            fetch(tiles_ref, b + depth_of_stage - held, place).start()

    block_scales[y] = coded_scale[...]
    slot_copies = {d: [] for d in range(RING)}
    for d in range(1, RING):
        slot_copies[0].append(send(coded_scale, block_scales.at[y], dy=d))
    chunk = BLOCK_ROWS // SLOT_CHUNKS

    def slot_group(d):
        slots[y, d] = coded[pick[d * RING + y]]
        for dy in range(1, RING):
            leaving[dy - 1, d] = coded[pick[d * RING + turn(y, dy)]]
        for r in range(SLOT_CHUNKS):
            part = pl.ds(r * chunk, chunk)
            for dy in (1, 3, 2):
                slot_copies[d].append(send(leaving.at[dy - 1, d, part], slots.at[y, d, part], dy=dy))

    slot_group(0)

    tile_at = [tile0, tile1, tile2, tile3]
    for t in range(n_tiles):
        fetch(tiles_ref, t, t).wait()
        code(t, tile0, t, tile_scale)
    tile_scales[0] = tile_scale[...]
    scale_copies = [send(tile_scale, tile_scales.at[RING - d], dz=d) for d in range(1, RING)]

    near_z[1, 0].wait_recv()
    far_z = {0: send(query_half(x, turn(z, 3), 0), query_half(x, turn(z, 3), 0), dz=1)}
    near_z[3, 1].wait_recv()
    far_z[1] = send(query_half(x, turn(z, 1), 1), query_half(x, turn(z, 1), 1), dz=3)
    near_z[1, 1].wait_recv()
    along_x[3] = query_sends(lambda h: query_half(x, turn(z, 3), h), turn(z, 3))
    near_z[3, 0].wait_recv()
    along_x[1] = query_sends(lambda h: query_half(x, turn(z, 1), h), turn(z, 1))

    train_relay(0)
    for d, copy in zip((3, 1, 2), train_z):
        copy.wait_recv()
        train_sends(d, train_part(y, d))
    near_tile = {}
    for k in range(n_tiles):
        near_tile[1, k] = send(tile0.at[k], tile3.at[k], dz=1)
        k = n_tiles - 1 - k
        near_tile[3, k] = send(tile0.at[k], tile1.at[k], dz=3)

    slot_group(3)

    def relay_x(d):
        at_z = turn(z, d)
        along_x[d][1, 0].wait_recv()
        first = send(query_half(turn(x, 3), at_z, 0), query_half(turn(x, 3), at_z, 0), dx=1)
        along_x[d][3, 1].wait_recv()
        second = send(query_half(turn(x, 1), at_z, 1), query_half(turn(x, 1), at_z, 1), dx=3)
        return first, second

    far_x = {0: relay_x(0)}

    far_z[0].wait_recv()
    far_z[1].wait_recv()
    along_x[2] = query_sends(lambda h: query_half(x, turn(z, 2), h), turn(z, 2))
    for d in (3, 1, 2):
        train_relay(d)
    slot_group(1)

    far_tile = []
    for k in range(n_tiles // 2):
        near_tile[1, k].wait_recv()
        far_tile.append(send(tile3.at[k], tile2.at[k], dz=1))
        k = n_tiles - 1 - k
        near_tile[3, k].wait_recv()
        far_tile.append(send(tile1.at[k], tile2.at[k], dz=3))
    slot_group(2)

    own[1].wait()

    def complete(d):
        along_x[d][1, 1].wait_recv()
        along_x[d][3, 0].wait_recv()
        far_x[d][0].wait_recv()
        far_x[d][1].wait_recv()
        view = queries.at[:, turn(z, d), :, my_part]
        return send(view, view, dc=1)

    out_copies, stay = [], []

    def score(d, from_core):
        to = turn(z, d)
        from_core.wait_recv()

        @pl.loop(0, RING)
        def _(k):
            value = lax.dot_general(
                trains[k], queries[k, to], (((1,), (1,)), ((), ())), preferred_element_type=jnp.float32
            )

            @pl.when(k == 0)
            def _():
                product[...] = value

            @pl.when(k > 0)
            def _():
                product[...] += value

        value = product[...]
        top = jnp.maximum(jnp.max(jnp.abs(value), axis=1, keepdims=True), 1e-30)
        ready[d] = jnp.round(value * (TOP / top)).astype(jnp.int32).astype(jnp.int16)
        ready_scale[d] = jnp.transpose(jnp.broadcast_to(top * (1.0 / TOP), (rows, 128)))[:8]
        if d == 0:
            stay.append(pltpu.make_async_copy(ready.at[0], out_ref.at[z], own_sem.at[2]))
            stay.append(pltpu.make_async_copy(ready_scale.at[0], out_scale_ref.at[z], own_sem.at[3]))
            for copy in stay:
                copy.start()
            return
        out_copies.append(send(ready_scale.at[d], out_scale_ref.at[z], dz=d))
        for h in range(2):
            part = pl.ds(h * half, half)
            out_copies.append(send(ready.at[d, part], out_ref.at[z, part], dz=d))

    step = 512

    def halves(codes):
        value = codes.astype(jnp.float32)
        high = value.astype(jnp.bfloat16)
        return high, (value - high.astype(jnp.float32)).astype(jnp.bfloat16)

    def line_of(lines, index):
        row = lax.broadcasted_iota(jnp.int32, lines.shape, 0)
        return jnp.sum(jnp.where(row == index, lines, 0.0), axis=0, keepdims=True)

    part_copies, back_copies = {}, []

    def exact_dots(d):
        if d in (1, 3):
            for k in range(n_tiles // 2):
                k = k if d == 1 else n_tiles - 1 - k
                near_tile[RING - d, k].wait_recv()
        if d == 2:
            for copy in far_tile:
                copy.wait_recv()
        for copy in slot_copies[d]:
            copy.wait_recv()

        @pl.loop(0, RING)
        def _(j):
            block, tile = pair_block[d * RING + j], pair_tile[d * RING + j]
            total = jnp.zeros((BLOCK_ROWS, BLOCK_ROWS), jnp.float32)
            for c in range(0, width, step):
                high, low = halves(slots[j, d, :, c : c + step])
                tile_high, tile_low = halves(tile_at[d][tile, :, c : c + step])
                for a, b in ((high, tile_high), (high, tile_low), (low, tile_high)):
                    total += lax.dot_general(a, b, (((1,), (1,)), ((), ())), preferred_element_type=jnp.float32)
            line = line_of(block_scales[j, :, 0], block)
            tall = jnp.transpose(jnp.broadcast_to(line, (BLOCK_ROWS, BLOCK_ROWS)))
            total = total * tall * line_of(tile_scales[d, :, 0], tile)
            parts[d, :, j] = total.reshape(n_ex, parts.shape[3], BLOCK_ROWS)

        part_copies[d] = []
        for k in range(1, n_ex):
            there = turn(x, k // 2) * 2 + (core + k % 2) % 2
            part_copies[d].append(send(parts.at[d, there], parts_in.at[d, k], dx=k // 2, dc=k % 2))

    def exact_sum(d):
        total = parts[d, ex]
        for k, copy in enumerate(part_copies[d], 1):
            copy.wait_recv()
            total += parts_in[d, k]
        if d == 0:
            back_in[z] = total
        else:
            back[d] = total
            back_copies.append(send(back.at[d], back_in.at[z], dz=d))

    from_core = {0: complete(0)}
    far_x[3] = relay_x(3)
    own[0].wait()
    for copy in far_y.values():
        copy.wait_recv()
    score(0, from_core[0])
    for copy in scale_copies:
        copy.wait_recv()
    exact_dots(0)
    from_core[3] = complete(3)
    far_x[1] = relay_x(1)
    score(3, from_core[3])
    from_core[1] = complete(1)
    far_x[2] = relay_x(2)
    score(1, from_core[1])
    from_core[2] = complete(2)
    score(2, from_core[2])
    exact_dots(3)
    exact_sum(0)
    exact_dots(1)
    exact_sum(3)
    exact_sum(1)
    exact_dots(2)

    exact_sum(2)
    for copy in back_copies:
        copy.wait_recv()
    for p in range(pairs):
        owner = wanted(qry, p) // held
        exact_ref[p] = back_in[owner % RING, owner // RING]

    for copy in out_copies:
        copy.wait_recv()
    for copy in stay:
        copy.wait()
    for copy in sent:
        copy.wait_send()


def decode_kernel(codes_ref, scale_ref, weight_ref, scores_ref):
    rows = codes_ref.shape[1]
    for m in range(codes_ref.shape[0]):
        line = scale_ref[m][:1] * weight_ref[m]
        tall = jnp.transpose(jnp.broadcast_to(line, (128, rows)))
        scores_ref[pl.ds(m * rows, rows)] = codes_ref[m].astype(jnp.float32) * tall[:, :1]


def local(train_proj, query_proj, out_weight, train_feat, query_feat, candidates):
    n_qry, n_ex = lax.axis_size("qry"), lax.axis_size("ex")
    width = train_feat.shape[1]
    held_blocks = train_feat.shape[0] // BLOCK_ROWS
    tiles_here = query_feat.shape[0] // BLOCK_ROWS
    pairs = tiles_here * CANDS
    depth = train_proj.shape[1]
    rows = train_proj.shape[0] // RING
    columns, part_depth = query_proj.shape
    share = BLOCK_ROWS // n_ex
    any_space, vmem = pl.BlockSpec(memory_space=pl.ANY), pl.BlockSpec(memory_space=pltpu.VMEM)
    dma = pltpu.SemaphoreType.DMA
    result, result_scale, exact = pl.pallas_call(
        main_kernel,
        out_shape=[
            jax.ShapeDtypeStruct((RING, rows, columns), jnp.int16),
            jax.ShapeDtypeStruct((RING, 8, rows), jnp.float32),
            jax.ShapeDtypeStruct((pairs, share, BLOCK_ROWS), jnp.float32),
        ],
        in_specs=[any_space] * 5,
        out_specs=[any_space, any_space, vmem],
        scratch_shapes=[
            pltpu.SMEM(candidates.shape[::-1], jnp.int32),
            pltpu.SMEM((n_qry,), jnp.int32),
            pltpu.SMEM((n_qry,), jnp.int32),
            pltpu.SMEM((n_qry,), jnp.int32),
            pltpu.VMEM((tiles_here, BLOCK_ROWS, width), jnp.float32),
            pltpu.VMEM((held_blocks, BLOCK_ROWS, width), jnp.int16),
            pltpu.VMEM((held_blocks, 1, BLOCK_ROWS), jnp.float32),
            pltpu.VMEM((tiles_here, BLOCK_ROWS, width), jnp.int16),
            pltpu.VMEM((tiles_here, BLOCK_ROWS, width), jnp.int16),
            pltpu.VMEM((tiles_here, BLOCK_ROWS, width), jnp.int16),
            pltpu.VMEM((tiles_here, BLOCK_ROWS, width), jnp.int16),
            pltpu.VMEM((tiles_here, 1, BLOCK_ROWS), jnp.float32),
            pltpu.VMEM((RING, held_blocks, 1, BLOCK_ROWS), jnp.float32),
            pltpu.VMEM((RING, tiles_here, 1, BLOCK_ROWS), jnp.float32),
            pltpu.VMEM((RING - 1, RING, BLOCK_ROWS, width), jnp.int16),
            pltpu.VMEM((RING, RING, BLOCK_ROWS, width), jnp.int16),
            pltpu.VMEM((RING, rows, RING * depth), jnp.bfloat16),
            pltpu.VMEM((RING, RING, columns, 2 * part_depth), jnp.bfloat16),
            pltpu.VMEM((rows, columns), jnp.float32),
            pltpu.VMEM((RING, rows, columns), jnp.int16),
            pltpu.VMEM((RING, 8, rows), jnp.float32),
            pltpu.VMEM((RING, n_ex, RING, share, BLOCK_ROWS), jnp.float32),
            pltpu.VMEM((RING, n_ex, RING, share, BLOCK_ROWS), jnp.float32),
            pltpu.VMEM((RING, RING, share, BLOCK_ROWS), jnp.float32),
            pltpu.VMEM((RING, RING, share, BLOCK_ROWS), jnp.float32),
            dma((tiles_here,)),
            dma((5,)),
            dma((COPIES,)),
            dma((COPIES,)),
        ],
        compiler_params=pltpu.CompilerParams(
            collective_id=0, has_side_effects=True, vmem_limit_bytes=61 * MIB
        ),
        name="main",
    )(
        candidates.T,
        train_proj.reshape(RING, rows, depth),
        query_proj,
        train_feat.reshape(held_blocks, BLOCK_ROWS, width),
        query_feat.reshape(tiles_here, BLOCK_ROWS, width),
    )
    scores = pl.pallas_call(
        decode_kernel,
        grid=(RING // MEMBERS,),
        in_specs=[
            pl.BlockSpec((MEMBERS, rows, columns), lambda i: (i, 0, 0)),
            pl.BlockSpec((MEMBERS, 8, rows), lambda i: (i, 0, 0)),
            pl.BlockSpec((MEMBERS, 1, rows), lambda i: (i, 0, 0)),
        ],
        out_specs=pl.BlockSpec((MEMBERS * rows, columns), lambda i: (i, 0)),
        out_shape=jax.ShapeDtypeStruct((RING * rows, columns), jnp.float32),
        compiler_params=pltpu.CompilerParams(vmem_limit_bytes=60 * MIB),
        name="decode",
    )(result, result_scale, out_weight.reshape(RING, 1, rows))
    return scores, exact.reshape(tiles_here, CANDS, share, BLOCK_ROWS)


def solution(mesh):
    placed = (P("ex", "qry"), P("qry", "ex"), P("ex"), P("qry", "ex"), P("qry", "ex"), P())
    return jax.shard_map(
        local,
        mesh=mesh,
        in_specs=placed,
        out_specs=(P("ex", "qry"), P("qry", None, "ex", None)),
        check_vma=False,
    )
```

```python
import jax
import jax.numpy as jnp
from jax import lax
from jax.experimental import pallas as pl
from jax.experimental.pallas import tpu as pltpu
from jax.sharding import PartitionSpec as P

BLOCK_ROWS = 128
CANDS = 2
RING = 4
SLOT_CHUNKS = 1
MEMBERS = 2
COPIES = 136
TOP = 32752.0
MESH = pl.DeviceIdType.MESH
MIB = 1 << 20


def main_kernel(
    cand_in_ref, train_ref, query_ref, blocks_ref, tiles_ref,
    out_ref, out_scale_ref, exact_ref,
    cand_ref, pick, pair_block, pair_tile, stage, coded, coded_scale, tile0, tile1, tile2, tile3, tile_scale,
    block_scales, tile_scales, leaving, slots, trains, queries, product, ready, ready_scale,
    parts, parts_in, back, back_in,
    stage_sem, own_sem, send_sem, recv_sem,
):
    ex, qry = lax.axis_index("ex"), lax.axis_index("qry")
    n_ex, n_qry = parts.shape[1], RING * RING
    x, core, y, z = ex // 2, ex % 2, qry // RING, qry % RING
    turn = lambda a, d: (a + d) % RING
    sent = []

    def send(src, dst, dx=0, dc=0, dy=0, dz=0):
        there = {"ex": turn(x, dx) * 2 + (core + dc) % 2, "qry": turn(y, dy) * RING + turn(z, dz)}
        k = len(sent)
        copy = pltpu.make_async_remote_copy(
            src_ref=src,
            dst_ref=dst,
            send_sem=send_sem.at[k],
            recv_sem=recv_sem.at[k],
            device_id=there,
            device_id_type=MESH,
        )
        copy.start()
        sent.append(copy)
        return copy

    rows, width = trains.shape[1], slots.shape[3]
    depth, part_depth = train_ref.shape[2], query_ref.shape[1]
    half = rows // 2
    my_depth = pl.ds(pl.multiple_of(z * depth, depth), depth)
    my_part = pl.ds(pl.multiple_of(core * part_depth, part_depth), part_depth)

    own = [
        pltpu.make_async_copy(train_ref.at[z], trains.at[y, :, my_depth], own_sem.at[0]),
        pltpu.make_async_copy(query_ref, queries.at[x, z, :, my_part], own_sem.at[1]),
    ]
    for copy in own:
        copy.start()
    cand_copy = pltpu.make_async_copy(cand_in_ref, cand_ref, own_sem.at[4])
    cand_copy.start()
    depth_of_stage = stage.shape[0]

    def fetch(source, index, place):
        return pltpu.make_async_copy(source.at[index], stage.at[place], stage_sem.at[place])

    for b in range(depth_of_stage):
        fetch(blocks_ref, b, b).start()

    barrier = pltpu.get_barrier_semaphore()
    for d in range(1, n_qry):
        there = turn(y, d // RING) * RING + turn(z, d % RING)
        pl.semaphore_signal(barrier, inc=1, device_id={"qry": there}, device_id_type=MESH)
    for d in range(1, n_ex):
        there = turn(x, d // 2) * 2 + (core + d % 2) % 2
        pl.semaphore_signal(barrier, inc=1, device_id={"ex": there}, device_id_type=MESH)
    pl.semaphore_wait(barrier, n_qry - 1 + n_ex - 1)

    def query_half(at_x, at_z, h):
        return queries.at[at_x, at_z, pl.ds(h * half, half), my_part]

    def query_sends(source, at_z):
        out = {}
        for h in range(2):
            for d in (1, 3):
                out[d, h] = send(source(h), query_half(x, at_z, h), dx=d)
        return out

    train_z = [
        send(train_ref.at[turn(z, d)], trains.at[y, :, my_depth], dz=d) for d in (1, 3, 2)
    ]

    near_z = {}
    for h in range(2):
        for d in (1, 3):
            near_z[d, h] = send(query_ref.at[pl.ds(h * half, half)], query_half(x, z, h), dz=d)
    along_x = {0: query_sends(lambda h: query_ref.at[pl.ds(h * half, half)], z)}
    near_y, far_y = {}, {}

    def train_part(at_y, d, first=0, many=None):
        columns = pl.ds(pl.multiple_of(turn(z, d) * depth, depth), depth)
        return trains.at[at_y, pl.ds(first, many or rows), columns]

    def train_sends(d, source):
        for dy in (1, 3):
            near_y[d, dy] = send(source, train_part(y, d), dy=dy)

    def train_relay(d):
        for dy, first in ((1, 0), (3, half)):
            near_y[d, dy].wait_recv()
            view = train_part(turn(y, RING - dy), d, first, half)
            far_y[d, dy] = send(view, view, dy=dy)

    train_sends(0, train_ref.at[z])

    held, n_tiles = coded.shape[0], tile0.shape[0]
    pairs = n_tiles * CANDS

    def wanted(q, p):
        return cand_ref[p % CANDS, q * n_tiles + p // CANDS]

    cand_copy.wait()

    @pl.loop(0, n_qry)
    def _(i):
        row, ring = i % RING, turn(z, i // RING)
        here, block, tile = jnp.int32(0), jnp.int32(0), jnp.int32(0)
        for p in range(pairs):
            place = wanted(row * RING + ring, p) - qry * held
            here = jnp.where((place >= 0) & (place < held), place, here)
            place = wanted(y * RING + ring, p) - (row * RING + z) * held
            match = (place >= 0) & (place < held)
            block = jnp.where(match, place, block)
            tile = jnp.where(match, p // CANDS, tile)
        pick[i] = here
        pair_block[i] = block
        pair_tile[i] = tile

    def code(place, to, at, line_to):
        whole = stage[place]
        top = jnp.maximum(jnp.max(jnp.abs(whole), axis=1, keepdims=True), 1e-30)
        to[at] = jnp.round(whole * (TOP / top)).astype(jnp.int32).astype(jnp.int16)
        wide = jnp.broadcast_to(top * (1.0 / TOP), (BLOCK_ROWS, BLOCK_ROWS))
        line_to[pl.ds(at, 1)] = jnp.transpose(wide)[:1].reshape(1, 1, BLOCK_ROWS)

    for b in range(held):
        place = b % depth_of_stage
        fetch(blocks_ref, b, place).wait()
        code(place, coded, b, coded_scale)
        if b + depth_of_stage < held:
            fetch(blocks_ref, b + depth_of_stage, place).start()
        else:
            fetch(tiles_ref, b + depth_of_stage - held, place).start()

    block_scales[y] = coded_scale[...]
    slot_copies = {d: [] for d in range(RING)}
    for d in range(1, RING):
        slot_copies[0].append(send(coded_scale, block_scales.at[y], dy=d))
    chunk = BLOCK_ROWS // SLOT_CHUNKS

    def slot_group(d):
        slots[y, d] = coded[pick[d * RING + y]]
        for dy in range(1, RING):
            leaving[dy - 1, d] = coded[pick[d * RING + turn(y, dy)]]
        for r in range(SLOT_CHUNKS):
            part = pl.ds(r * chunk, chunk)
            for dy in (1, 3, 2):
                slot_copies[d].append(send(leaving.at[dy - 1, d, part], slots.at[y, d, part], dy=dy))

    slot_group(0)

    tile_at = [tile0, tile1, tile2, tile3]
    for t in range(n_tiles):
        fetch(tiles_ref, t, t).wait()
        code(t, tile0, t, tile_scale)
    tile_scales[0] = tile_scale[...]
    scale_copies = [send(tile_scale, tile_scales.at[RING - d], dz=d) for d in range(1, RING)]

    near_z[1, 0].wait_recv()
    far_z = {0: send(query_half(x, turn(z, 3), 0), query_half(x, turn(z, 3), 0), dz=1)}
    near_z[3, 1].wait_recv()
    far_z[1] = send(query_half(x, turn(z, 1), 1), query_half(x, turn(z, 1), 1), dz=3)
    near_z[1, 1].wait_recv()
    along_x[3] = query_sends(lambda h: query_half(x, turn(z, 3), h), turn(z, 3))
    near_z[3, 0].wait_recv()
    along_x[1] = query_sends(lambda h: query_half(x, turn(z, 1), h), turn(z, 1))

    train_relay(0)
    for d, copy in zip((3, 1, 2), train_z):
        copy.wait_recv()
        train_sends(d, train_part(y, d))
    near_tile = {}
    for k in range(n_tiles):
        near_tile[1, k] = send(tile0.at[k], tile3.at[k], dz=1)
        k = n_tiles - 1 - k
        near_tile[3, k] = send(tile0.at[k], tile1.at[k], dz=3)

    slot_group(3)

    def relay_x(d):
        at_z = turn(z, d)
        along_x[d][1, 0].wait_recv()
        first = send(query_half(turn(x, 3), at_z, 0), query_half(turn(x, 3), at_z, 0), dx=1)
        along_x[d][3, 1].wait_recv()
        second = send(query_half(turn(x, 1), at_z, 1), query_half(turn(x, 1), at_z, 1), dx=3)
        return first, second

    far_x = {0: relay_x(0)}

    far_z[0].wait_recv()
    far_z[1].wait_recv()
    along_x[2] = query_sends(lambda h: query_half(x, turn(z, 2), h), turn(z, 2))
    for d in (3, 1, 2):
        train_relay(d)
    slot_group(1)

    slot_group(2)
    far_tile = []
    for k in range(n_tiles // 2):
        near_tile[1, k].wait_recv()
        far_tile.append(send(tile3.at[k], tile2.at[k], dz=1))
        k = n_tiles - 1 - k
        near_tile[3, k].wait_recv()
        far_tile.append(send(tile1.at[k], tile2.at[k], dz=3))

    own[1].wait()

    def complete(d):
        along_x[d][1, 1].wait_recv()
        along_x[d][3, 0].wait_recv()
        far_x[d][0].wait_recv()
        far_x[d][1].wait_recv()
        view = queries.at[:, turn(z, d), :, my_part]
        return send(view, view, dc=1)

    out_copies, stay = [], []

    def score(d, from_core):
        to = turn(z, d)
        from_core.wait_recv()

        @pl.loop(0, RING)
        def _(k):
            value = lax.dot_general(
                trains[k], queries[k, to], (((1,), (1,)), ((), ())), preferred_element_type=jnp.float32
            )

            @pl.when(k == 0)
            def _():
                product[...] = value

            @pl.when(k > 0)
            def _():
                product[...] += value

        value = product[...]
        top = jnp.maximum(jnp.max(jnp.abs(value), axis=1, keepdims=True), 1e-30)
        ready[d] = jnp.round(value * (TOP / top)).astype(jnp.int32).astype(jnp.int16)
        ready_scale[d] = jnp.transpose(jnp.broadcast_to(top * (1.0 / TOP), (rows, 128)))[:8]
        if d == 0:
            stay.append(pltpu.make_async_copy(ready.at[0], out_ref.at[z], own_sem.at[2]))
            stay.append(pltpu.make_async_copy(ready_scale.at[0], out_scale_ref.at[z], own_sem.at[3]))
            for copy in stay:
                copy.start()
            return
        out_copies.append(send(ready_scale.at[d], out_scale_ref.at[z], dz=d))
        for h in range(2):
            part = pl.ds(h * half, half)
            out_copies.append(send(ready.at[d, part], out_ref.at[z, part], dz=d))

    step = 512

    def halves(codes):
        value = codes.astype(jnp.float32)
        high = value.astype(jnp.bfloat16)
        return high, (value - high.astype(jnp.float32)).astype(jnp.bfloat16)

    def line_of(lines, index):
        row = lax.broadcasted_iota(jnp.int32, lines.shape, 0)
        return jnp.sum(jnp.where(row == index, lines, 0.0), axis=0, keepdims=True)

    part_copies, back_copies = {}, []

    def exact_dots(d):
        if d in (1, 3):
            for k in range(n_tiles // 2):
                k = k if d == 1 else n_tiles - 1 - k
                near_tile[RING - d, k].wait_recv()
        if d == 2:
            for copy in far_tile:
                copy.wait_recv()
        for copy in slot_copies[d]:
            copy.wait_recv()

        @pl.loop(0, RING)
        def _(j):
            block, tile = pair_block[d * RING + j], pair_tile[d * RING + j]
            total = jnp.zeros((BLOCK_ROWS, BLOCK_ROWS), jnp.float32)
            for c in range(0, width, step):
                high, low = halves(slots[j, d, :, c : c + step])
                tile_high, tile_low = halves(tile_at[d][tile, :, c : c + step])
                for a, b in ((high, tile_high), (high, tile_low), (low, tile_high)):
                    total += lax.dot_general(a, b, (((1,), (1,)), ((), ())), preferred_element_type=jnp.float32)
            line = line_of(block_scales[j, :, 0], block)
            tall = jnp.transpose(jnp.broadcast_to(line, (BLOCK_ROWS, BLOCK_ROWS)))
            total = total * tall * line_of(tile_scales[d, :, 0], tile)
            parts[d, :, j] = total.reshape(n_ex, parts.shape[3], BLOCK_ROWS)

        part_copies[d] = []
        for k in range(1, n_ex):
            there = turn(x, k // 2) * 2 + (core + k % 2) % 2
            part_copies[d].append(send(parts.at[d, there], parts_in.at[d, k], dx=k // 2, dc=k % 2))

    def exact_sum(d):
        total = parts[d, ex]
        for k, copy in enumerate(part_copies[d], 1):
            copy.wait_recv()
            total += parts_in[d, k]
        if d == 0:
            back_in[z] = total
        else:
            back[d] = total
            back_copies.append(send(back.at[d], back_in.at[z], dz=d))

    from_core = {0: complete(0)}
    far_x[3] = relay_x(3)
    own[0].wait()
    for copy in far_y.values():
        copy.wait_recv()
    score(0, from_core[0])
    for copy in scale_copies:
        copy.wait_recv()
    exact_dots(0)
    from_core[3] = complete(3)
    far_x[1] = relay_x(1)
    score(3, from_core[3])
    from_core[1] = complete(1)
    far_x[2] = relay_x(2)
    score(1, from_core[1])
    from_core[2] = complete(2)
    score(2, from_core[2])
    exact_dots(3)
    exact_sum(0)
    exact_dots(1)
    exact_sum(3)
    exact_sum(1)
    exact_dots(2)

    exact_sum(2)
    for copy in back_copies:
        copy.wait_recv()
    for p in range(pairs):
        owner = wanted(qry, p) // held
        exact_ref[p] = back_in[owner % RING, owner // RING]

    for copy in out_copies:
        copy.wait_recv()
    for copy in stay:
        copy.wait()
    for copy in sent:
        copy.wait_send()


def decode_kernel(codes_ref, scale_ref, weight_ref, scores_ref):
    rows = codes_ref.shape[1]
    for m in range(codes_ref.shape[0]):
        line = scale_ref[m][:1] * weight_ref[m]
        tall = jnp.transpose(jnp.broadcast_to(line, (128, rows)))
        scores_ref[pl.ds(m * rows, rows)] = codes_ref[m].astype(jnp.float32) * tall[:, :1]


def local(train_proj, query_proj, out_weight, train_feat, query_feat, candidates):
    n_qry, n_ex = lax.axis_size("qry"), lax.axis_size("ex")
    width = train_feat.shape[1]
    held_blocks = train_feat.shape[0] // BLOCK_ROWS
    tiles_here = query_feat.shape[0] // BLOCK_ROWS
    pairs = tiles_here * CANDS
    depth = train_proj.shape[1]
    rows = train_proj.shape[0] // RING
    columns, part_depth = query_proj.shape
    share = BLOCK_ROWS // n_ex
    any_space, vmem = pl.BlockSpec(memory_space=pl.ANY), pl.BlockSpec(memory_space=pltpu.VMEM)
    dma = pltpu.SemaphoreType.DMA
    result, result_scale, exact = pl.pallas_call(
        main_kernel,
        out_shape=[
            jax.ShapeDtypeStruct((RING, rows, columns), jnp.int16),
            jax.ShapeDtypeStruct((RING, 8, rows), jnp.float32),
            jax.ShapeDtypeStruct((pairs, share, BLOCK_ROWS), jnp.float32),
        ],
        in_specs=[any_space] * 5,
        out_specs=[any_space, any_space, vmem],
        scratch_shapes=[
            pltpu.SMEM(candidates.shape[::-1], jnp.int32),
            pltpu.SMEM((n_qry,), jnp.int32),
            pltpu.SMEM((n_qry,), jnp.int32),
            pltpu.SMEM((n_qry,), jnp.int32),
            pltpu.VMEM((tiles_here, BLOCK_ROWS, width), jnp.float32),
            pltpu.VMEM((held_blocks, BLOCK_ROWS, width), jnp.int16),
            pltpu.VMEM((held_blocks, 1, BLOCK_ROWS), jnp.float32),
            pltpu.VMEM((tiles_here, BLOCK_ROWS, width), jnp.int16),
            pltpu.VMEM((tiles_here, BLOCK_ROWS, width), jnp.int16),
            pltpu.VMEM((tiles_here, BLOCK_ROWS, width), jnp.int16),
            pltpu.VMEM((tiles_here, BLOCK_ROWS, width), jnp.int16),
            pltpu.VMEM((tiles_here, 1, BLOCK_ROWS), jnp.float32),
            pltpu.VMEM((RING, held_blocks, 1, BLOCK_ROWS), jnp.float32),
            pltpu.VMEM((RING, tiles_here, 1, BLOCK_ROWS), jnp.float32),
            pltpu.VMEM((RING - 1, RING, BLOCK_ROWS, width), jnp.int16),
            pltpu.VMEM((RING, RING, BLOCK_ROWS, width), jnp.int16),
            pltpu.VMEM((RING, rows, RING * depth), jnp.bfloat16),
            pltpu.VMEM((RING, RING, columns, 2 * part_depth), jnp.bfloat16),
            pltpu.VMEM((rows, columns), jnp.float32),
            pltpu.VMEM((RING, rows, columns), jnp.int16),
            pltpu.VMEM((RING, 8, rows), jnp.float32),
            pltpu.VMEM((RING, n_ex, RING, share, BLOCK_ROWS), jnp.float32),
            pltpu.VMEM((RING, n_ex, RING, share, BLOCK_ROWS), jnp.float32),
            pltpu.VMEM((RING, RING, share, BLOCK_ROWS), jnp.float32),
            pltpu.VMEM((RING, RING, share, BLOCK_ROWS), jnp.float32),
            dma((tiles_here,)),
            dma((5,)),
            dma((COPIES,)),
            dma((COPIES,)),
        ],
        compiler_params=pltpu.CompilerParams(
            collective_id=0, has_side_effects=True, vmem_limit_bytes=61 * MIB
        ),
        name="main",
    )(
        candidates.T,
        train_proj.reshape(RING, rows, depth),
        query_proj,
        train_feat.reshape(held_blocks, BLOCK_ROWS, width),
        query_feat.reshape(tiles_here, BLOCK_ROWS, width),
    )
    scores = pl.pallas_call(
        decode_kernel,
        grid=(RING // MEMBERS,),
        in_specs=[
            pl.BlockSpec((MEMBERS, rows, columns), lambda i: (i, 0, 0)),
            pl.BlockSpec((MEMBERS, 8, rows), lambda i: (i, 0, 0)),
            pl.BlockSpec((MEMBERS, 1, rows), lambda i: (i, 0, 0)),
        ],
        out_specs=pl.BlockSpec((MEMBERS * rows, columns), lambda i: (i, 0)),
        out_shape=jax.ShapeDtypeStruct((RING * rows, columns), jnp.float32),
        compiler_params=pltpu.CompilerParams(vmem_limit_bytes=60 * MIB),
        name="decode",
    )(result, result_scale, out_weight.reshape(RING, 1, rows))
    return scores, exact.reshape(tiles_here, CANDS, share, BLOCK_ROWS)


def solution(mesh):
    placed = (P("ex", "qry"), P("qry", "ex"), P("ex"), P("qry", "ex"), P("qry", "ex"), P())
    return jax.shard_map(
        local,
        mesh=mesh,
        in_specs=placed,
        out_specs=(P("ex", "qry"), P("qry", None, "ex", None)),
        check_vma=False,
    )
```
